512 devices in a mesh: gx: 8 (over z), gy: 8 (over y_lo, core), gz: 8 (over x, y_hi).
Axes of the slice: x: 4, y: 8 (y_hi: 2, y_lo: 4; y = y_hi * 4 + y_lo), z: 8, core: 2. Of those that a mesh axis runs over, the one named last changes fastest.
Arguments:
- charges: float32 [128, 128, 1024], P('gx', 'gy', 'gz'), may hold values from -6 to 6
- exponents: float32 [2, 4], replicated, may hold values from 0.01 to 1
- amplitudes: float32 [2, 4], replicated, may hold values from 0.25 to 1
- top_x: float32 [8, 8], replicated, may hold values from -1 to 1
- top_y: float32 [8, 8], replicated, may hold values from -1 to 1
- top_z: float32 [64, 64], replicated, may hold values from -0.375 to 0.375
Outputs:
- potential: float32 [128, 128, 1024], P('gx', 'gy', 'gz')
The draws below stay inside these ranges and needn't reach their ends.
All inputs are finite; a program needn't handle non-finite values.
Results may differ from the reference program's by a relative error of at most 0.0003.
Values sent between devices are 32-bit elements; how exact they have to be, the bound alone decides.
A program may use at most 64 MiB of HBM per device.

```python
import math
import jax
import jax.numpy as jnp
from jax import lax

GAUSSIANS = 4
REACH = 8
NX = 128
NY = 128
NZ = 1024
TX = 8
TY = 8
TZ = 64


def steps_of(stream_key, extent, cuts, smallest, largest):
    level, own = 1.0, jax.random.fold_in(stream_key, 6)
    for axis_at, blocks in cuts:
        steps = jnp.exp(jax.random.uniform(jax.random.fold_in(own, axis_at), (blocks,), jnp.float32, smallest / len(cuts), largest / len(cuts)))
        level = level * jnp.repeat(steps, extent[axis_at] // blocks).reshape([-1 if axis == axis_at else 1 for axis in range(len(extent))])
    return level


def normal_values(key, dims, spread, limit, cuts=(), kind=jnp.bfloat16):
    drawn = jax.random.normal(key, dims, jnp.float32) * spread
    if len(cuts) > 0:
        drawn = steps_of(key, dims, cuts, -0.22, 0.18) * drawn
    return jnp.clip(drawn, min=-limit, max=limit).astype(kind)


def setup_inputs(seed: int = 0) -> dict:
    keys = jax.random.split(jax.random.key(seed), 7)
    return {
        "charges": normal_values(keys[0], (NX, NY, NZ), 1.0, 6.0, ((0, 8), (1, 8), (2, 8)), jnp.float32),
        "exponents": jnp.clip(jnp.exp(jax.random.uniform(keys[1], (2, GAUSSIANS), jnp.float32, math.log(0.01), math.log(1.0))), 0.01, 1.0),
        "amplitudes": jnp.clip(jnp.exp(jax.random.uniform(keys[2], (2, GAUSSIANS), jnp.float32, math.log(0.25), math.log(1.0))), 0.25, 1.0),
        "top_x": normal_values(keys[3], (TX, TX), (4 * TX) ** -0.5, 1.0, (), jnp.float32),
        "top_y": normal_values(keys[4], (TY, TY), (4 * TY) ** -0.5, 1.0, (), jnp.float32),
        "top_z": normal_values(keys[5], (TZ, TZ), (4 * TZ) ** -0.5, 0.375, (), jnp.float32),
    }


HIGHEST = lax.Precision.HIGHEST


def gauss_taps(exponents):
    offsets = jnp.arange(-REACH, REACH + 1).astype(jnp.float32)
    weights = jnp.exp(-exponents[..., None] * offsets * offsets)
    return weights / jnp.sum(weights, axis=-1, keepdims=True)


def smooth_axis(field, tap_row, axis):
    summed = jnp.zeros_like(field)
    for offset in range(2 * REACH + 1):
        summed = summed + tap_row[offset] * jnp.roll(field, REACH - offset, axis)
    return summed


def gauss_term(field, tap_table, weights):
    summed = jnp.zeros_like(field)
    for term in range(GAUSSIANS):
        smoothed = smooth_axis(field, tap_table[term], 2)
        smoothed = smooth_axis(smoothed, tap_table[term], 1)
        smoothed = smooth_axis(smoothed, tap_table[term], 0)
        summed = summed + weights[term] * smoothed
    return summed


def restrict_axis(field, axis):
    length = field.shape[axis]
    summed = (jnp.roll(field, 1, axis) + 3.0 * field + 3.0 * jnp.roll(field, -1, axis) + jnp.roll(field, -2, axis)) * 0.25
    return lax.slice_in_dim(summed, 0, length, 2, axis)


def restrict_three(field):
    return restrict_axis(restrict_axis(restrict_axis(field, 0), 1), 2)


def prolong_axis(coarse, axis):
    even_cells = 0.75 * coarse + 0.25 * jnp.roll(coarse, 1, axis)
    odd_cells = 0.75 * coarse + 0.25 * jnp.roll(coarse, -1, axis)
    stacked = jnp.stack([even_cells, odd_cells], axis=axis + 1)
    sizes = list(coarse.shape)
    sizes[axis] = sizes[axis] * 2
    return stacked.reshape(sizes)


def prolong_three(field):
    return prolong_axis(prolong_axis(prolong_axis(field, 0), 1), 2)


def reference(charges, exponents, amplitudes, top_x, top_y, top_z):
    tap_table = gauss_taps(exponents)
    level_one = restrict_three(charges)
    level_two = restrict_three(level_one)
    level_three = restrict_three(level_two)
    level_four = restrict_three(level_three)
    phi_four = jnp.einsum('ia,abc->ibc', top_x, level_four, precision=HIGHEST)
    phi_four = jnp.einsum('jb,ibc->ijc', top_y, phi_four, precision=HIGHEST)
    phi_four = jnp.einsum('kc,ijc->ijk', top_z, phi_four, precision=HIGHEST)
    phi_two = prolong_three(prolong_three(phi_four))
    phi_one = gauss_term(level_one, tap_table[1], amplitudes[1]) + prolong_three(phi_two)
    return gauss_term(charges, tap_table[0], amplitudes[0]) + prolong_three(phi_one)
```

```python
import functools

import jax
import jax.numpy as jnp
import numpy as np
from jax import lax
from jax.experimental import pallas as pl
from jax.experimental.pallas import tpu as pltpu
from jax.sharding import PartitionSpec as P

MESH = pl.DeviceIdType.MESH
TERMS = 4
REACH = 8
F32 = jnp.float32
BF16 = jnp.bfloat16
NEAR = [(dx, dy) for dx in (-1, 0, 1) for dy in (-1, 0, 1) if (dx, dy) != (0, 0)]
AXES = ("gx", "gy", "gz")


def spline_np(off):
    off = np.asarray(off)
    return np.where((off == 1) | (off == 2), 0.75, np.where((off == 0) | (off == 3), 0.25, 0.0))


def composite_np(levels):
    box = np.ones(2**levels)
    return np.convolve(np.convolve(box, box), box) / 4.0**levels


def composite_at(levels, fine, cell):
    taps = composite_np(levels)
    off = fine - (cell * 2**levels - (2**levels - 1))
    return np.where((off >= 0) & (off < len(taps)), taps[np.clip(off, 0, len(taps) - 1)], 0.0)


def tables():
    x = np.arange(16)[:, None]
    i = np.arange(10)[None, :]
    px = spline_np(x - 2 * i + 3)
    j = np.arange(16)[None, :]
    py = np.where(j < 10, spline_np(x - 2 * j + 3), 0.0)
    pp = np.einsum("xi,yj->xyij", px, py).reshape(256, 160)
    row = np.arange(128)[:, None]
    lane = np.arange(128)[None, :]
    rt = spline_np(lane - 2 * row + 3)
    m = np.arange(24)[:, None]
    yi = np.arange(32)[None, :]
    ry = np.where(m < 10, spline_np(yi - 2 * m - 5), np.where(m >= 16, spline_np(yi - 2 * m + 23), 0.0))
    ry2 = np.concatenate([ry, ry], axis=1)
    r = np.arange(16)
    a, b = r >> 2, r & 3
    wa = composite_at(4, np.arange(16)[None, :], a[:, None] - 1) * (a < 3)[:, None]
    wb = composite_at(4, np.arange(16)[None, :], b[:, None] - 1) * (b < 3)[:, None]
    w9 = np.einsum("rx,ry->rxy", wa, wb).reshape(16, 256)
    ci = np.arange(10)[:, None] - 1
    cj = np.arange(16)[:, None] - 1
    pa = composite_at(3, ci, a[None, :] - 1) * (a < 3)[None, :]
    pb = composite_at(3, cj, b[None, :] - 1) * (b < 3)[None, :] * (np.arange(16) < 10)[:, None]
    p3 = np.einsum("ir,jr->ijr", pa, pb).reshape(160, 16)
    mm = np.arange(32)[:, None]
    zf = np.arange(128)[None, :]
    cell = np.where(mm < 16, 55 + mm, mm - 17)
    edge = np.where((mm % 16) < 10, spline_np(zf - 2 * cell + 1), 0.0)
    t = np.arange(16)[:, None]
    sel = (zf == np.where(t < 8, 120 + t, t - 8)).astype(np.float64)
    bf = lambda v: np.asarray(v, np.float32).astype(jnp.bfloat16)
    fl = lambda v: np.asarray(v, np.float32)
    return [bf(pp), bf(rt), bf(rt.T), bf(ry2), fl(w9), fl(p3), bf(edge), bf(sel)]


def split(v):
    hi = v.astype(BF16)
    return hi, (v - hi.astype(F32)).astype(BF16)


def dot(a, b, dims=((1,), (0,))):
    return lax.dot_general(a, b, (dims, ((), ())), preferred_element_type=F32)


def dot3(a, b, dims=((1,), (0,))):
    ah, al = split(a)
    bh, bl = split(b)
    return dot(ah, bh, dims) + dot(ah, bl, dims) + dot(al, bh, dims)


def iota(shape, dim):
    return lax.broadcasted_iota(jnp.int32, shape, dim)


def by_term(values, index):
    out = jnp.where(index == 0, values[0], values[1])
    for t in range(2, TERMS):
        out = jnp.where(index == t, values[t], out)
    return out


def composite4(fine, cell):
    off = fine - (cell * 16 - 15)

    def pairs(shift):
        m = jnp.maximum(off + shift, 0).astype(F32)
        return m * (m - 1.0) * 0.5

    return (pairs(2) - 3.0 * pairs(-14) + 3.0 * pairs(-30) - pairs(-46)) * (1.0 / 256.0)


def kernel(
    sizes,
    charges, exps, amps, top_x, top_y, top_z,
    c_pp, c_rt, c_r, c_ry, c_w9, c_p3, c_edge, c_sel,
    out,
    ext, v0, y0, fext, q2, v1, y1,
    rx1, rx2, rx3, tx1, tx2, tx3,
    zs0, zs1, zr0, zr1,
    taps, inv,
    a_send, a_recv, b_send, b_recv, t_send, t_recv, z_send, z_recv,
):
    nx, ny, nz = sizes
    me = [lax.axis_index(axis) for axis in AXES]
    gx, gy, gz = me

    def at(dx, dy, dz):
        return (lax.rem(gx + dx + nx, nx), lax.rem(gy + dy + ny, ny), lax.rem(gz + dz + nz, nz))

    partners = [(dx, dy, 0) for dx, dy in NEAR]
    partners += [(o, 0, 0) for o in range(2, nx - 1)]
    partners += [(0, o, 0) for o in range(2, ny - 1)]
    partners += [(0, 0, o) for o in range(1, nz)]
    barrier = pltpu.get_barrier_semaphore()
    for p in partners:
        pl.semaphore_signal(barrier, inc=1, device_id=at(*p), device_id_type=MESH)

    ext[8:24, 8:24, :] = charges[...]
    flat = charges[...].reshape(256, 128)
    part = dot3(c_w9[...], flat)
    zi = iota((128, 128), 0)
    lane = iota((128, 128), 1)
    slot = lane & 15
    place = jnp.where(((lane >> 4) == gz) & (slot < 10), composite4(zi, slot - 1), 0.0)
    tx1[...] = dot3(part, place)
    rx1[0] = tx1[...]
    pl.semaphore_wait(barrier, len(partners))

    def remote(src, dst, send, recv, where):
        return pltpu.make_async_remote_copy(
            src_ref=src, dst_ref=dst, send_sem=send, recv_sem=recv, device_id=at(*where), device_id_type=MESH
        )

    def top_copies(step, src, dst):
        shift = [(1, 0, 0), (0, 1, 0), (0, 0, 1)][step]
        return [
            remote(
                src, dst.at[o], t_send.at[step * 8 + o], t_recv.at[step * 8 + o],
                (shift[0] * o, shift[1] * o, shift[2] * o),
            )
            for o in range(1, sizes[step])
        ]

    source_a = {-1: pl.ds(8, 8), 0: pl.ds(8, 16), 1: pl.ds(16, 8)}
    target_a = {-1: pl.ds(24, 8), 0: pl.ds(8, 16), 1: pl.ds(0, 8)}
    copies_t1 = top_copies(0, tx1, rx1)
    copies_a = [
        remote(
            ext.at[source_a[dx], source_a[dy], :], ext.at[target_a[dx], target_a[dy], :],
            a_send.at[n], a_recv.at[n], (dx, dy, 0),
        )
        for n, (dx, dy) in enumerate(NEAR)
    ]
    for copy in copies_t1:
        copy.start()
    for copy in copies_a:
        copy.start()

    for level in range(2):
        for r in range(TERMS):
            e = jnp.full((8, 128), exps[level, r], F32)
            weights = [jnp.exp(-e * float(k * k)) for k in range(REACH + 1)]
            total = weights[1]
            for k in range(2, REACH + 1):
                total = total + weights[k]
            inverse = 1.0 / (1.0 + 2.0 * total)
            inv[level * TERMS + r] = inverse
            for k in range(REACH + 1):
                taps[(level * TERMS + r) * 9 + k] = weights[k] * inverse * amps[level, r]

    def band(level, term, offset):
        if isinstance(term, int):
            e = exps[level, term]
            scale = inv[level * TERMS + term][0:1, 0:1]
        else:
            e = by_term([exps[level, t] for t in range(TERMS)], term)
            scale = by_term([inv[level * TERMS + t][0:1, 0:1] for t in range(TERMS)], term)
        far = offset.astype(F32)
        return jnp.where(jnp.abs(offset) <= REACH, jnp.exp(-e * (far * far)) * scale, 0.0)

    def tripled(matrix, copy_at):
        hi = matrix.astype(BF16)
        lo = (matrix - hi.astype(F32)).astype(BF16)
        return jnp.where(copy_at == 1, lo.astype(F32), hi.astype(F32)).astype(BF16)

    row = iota((64, 96), 0)
    col = iota((64, 96), 1)
    col32 = col & 31
    band_y0 = tripled(band(0, row >> 4, col32 - 8 - (row & 15)), col >> 5)
    where1 = jnp.where(col32 < 18, col32 - 9, jnp.where(col32 >= 24, col32 - 15, 1000))
    off1 = jnp.where((row & 15) < 10, where1 - ((row & 15) - 1), 1000)
    band_y1 = tripled(band(1, row >> 4, off1), col >> 5)

    def tops(table, own, shape_sizes, first):
        r8 = iota((16, 8), 0)
        p8 = iota((16, 8), 1)
        c8 = iota((8, 128), 0)
        l8 = iota((8, 128), 1)
        rr = iota((16, 128), 0)
        ll = iota((16, 128), 1)
        if first:
            mine, theirs = r8 >> 2, (l8 & 15) >> 2
            same = (rr & 3) == (ll & 3)
        else:
            mine, theirs = r8 & 3, l8 & 3
            same = (rr >> 2) == ((ll & 15) >> 2)
        pick_rows = (p8 == ((own + mine + 7) & 7)).astype(F32)
        pick_cols = (c8 == ((own - (l8 >> 4) + theirs + 15) & 7)).astype(F32)
        whole = dot3(dot3(pick_rows, table), pick_cols)
        valid = ((rr >> 2) < 3) & ((rr & 3) < 3) & (((ll & 15) >> 2) < 3) & ((ll & 3) < 3)
        return jnp.where(same & valid, whole, 0.0)

    mix_x = tops(top_x[...], gx, sizes, True)
    for n, copy in enumerate(copies_t1):
        copy.wait_recv()
    tx2[...] = dot3(mix_x, rx1[...].reshape(128, 128))
    rx2[0] = tx2[...]
    copies_t2 = top_copies(1, tx2, rx2)
    for copy in copies_t2:
        copy.start()

    for copy in copies_a:
        copy.wait_recv()

    for i in range(10):
        rx = 0.25 * (ext[2 * i + 5] + ext[2 * i + 8]) + 0.75 * (ext[2 * i + 6] + ext[2 * i + 7])
        hi, lo = split(rx)
        cells = dot(c_ry[...], jnp.concatenate([hi, lo], axis=0))
        fext[8 + i, 8:24, :] = cells[0:16]
        q2[i] = cells[16:24]

    xs = {-1: pl.ds(10, 8), 0: pl.ds(8, 10), 1: pl.ds(8, 8)}
    xd = {-1: pl.ds(18, 8), 0: pl.ds(8, 10), 1: pl.ds(0, 8)}
    yd = {-1: pl.ds(24, 8), 0: pl.ds(8, 16), 1: pl.ds(0, 8)}
    copies_b = []
    for n, (dx, dy) in enumerate(NEAR):
        if dy == -1:
            src = q2.at[pl.ds(xs[dx].start - 8, xs[dx].size)]
        else:
            src = fext.at[xs[dx], pl.ds(8, 16 if dy == 0 else 8), :]
        copies_b.append(
            remote(src, fext.at[xd[dx], yd[dy], :], b_send.at[n], b_recv.at[n], (dx, dy, 0))
        )
    for copy in copies_b:
        copy.start()

    mix_y = tops(top_y[...], gy, sizes, False)
    for copy in copies_t2:
        copy.wait_recv()
    tx3[...] = dot3(mix_y, rx2[...].reshape(128, 128))
    rx3[0] = tx3[...]
    copies_t3 = top_copies(2, tx3, rx3)
    for copy in copies_t3:
        copy.start()

    def smooth_y(source, band_y, target, at_x):
        hi, lo = split(source[at_x])
        target[at_x] = dot(band_y, jnp.concatenate([hi, hi, lo], axis=0))

    def level0_y(step, carry):
        for u in range(8):
            smooth_y(ext, band_y0, v0, step * 8 + u)
        return carry

    lax.fori_loop(0, 4, level0_y, 0)

    def smooth_x(source, target, level, count, stride):
        for r in range(TERMS):
            w = [taps[(level * TERMS + r) * 9 + k] for k in range(9)]
            for half in range(2):
                rows = slice(r * 16 + half * 8, r * 16 + half * 8 + 8)
                for x in range(count):
                    acc = w[0] * source[x + 8, rows, :]
                    for k in range(1, 9):
                        acc = acc + w[k] * (source[x + 8 - k, rows, :] + source[x + 8 + k, rows, :])
                    target[x * 16 + half * 8 : x * 16 + half * 8 + 8, r * 128 : r * 128 + 128] = acc

    smooth_x(v0, y0, 0, 16, 16)

    zi = iota((128, 128), 0)
    zo = iota((128, 128), 1)
    band_z0 = jnp.concatenate([band(0, r, zi - zo) for r in range(TERMS)], axis=0)
    h_row = iota((16, 128), 0)
    h_lane = iota((16, 128), 1)
    h_out = jnp.where(h_row < 8, h_row - 8, h_row + 120)
    edge_z0 = jnp.concatenate([band(0, r, h_lane - h_out) for r in range(TERMS)], axis=1)
    y0h, y0l = split(y0[...])
    eh, el = split(edge_z0)
    nt = ((1,), (1,))
    zs0[...] = dot(eh, y0h, nt) + dot(eh, y0l, nt) + dot(el, y0h, nt)
    left, right = (0, 0, -1), (0, 0, 1)
    copies_z0 = [
        remote(zs0.at[pl.ds(0, 8)], zr0.at[pl.ds(0, 8)], z_send.at[0], z_recv.at[0], left),
        remote(zs0.at[pl.ds(8, 8)], zr0.at[pl.ds(8, 8)], z_send.at[1], z_recv.at[1], right),
    ]
    for copy in copies_z0:
        copy.start()
    bh, bl = split(band_z0)
    out[...] = (dot(y0h, bh) + dot(y0h, bl) + dot(y0l, bh)).reshape(16, 16, 128)

    g_row = iota((32, 128), 0)
    g_cell = iota((32, 128), 1) - 1
    g_out = jnp.where(g_row < 16, g_row - 9, g_row + 47)
    g_out = jnp.where((g_row & 15) < 10, g_out, 1000)
    mains, edges = [], []
    for r in range(TERMS):
        gh, gl = split(band(1, r, zi - zo))
        ch, cl = split(dot(c_r[...], gh) + dot(c_r[...], gl))
        mains.append(dot(ch, c_rt[...]) + dot(cl, c_rt[...]))
        eh, el = split(band(1, r, g_cell - g_out))
        edges.append(dot(eh, c_rt[...]) + dot(el, c_rt[...]))
    main_h, main_l = split(jnp.concatenate(mains, axis=0))
    edge_h, edge_l = split(jnp.concatenate(edges, axis=1))

    p_at = iota((128, 64), 1)
    z_at = iota((128, 64), 0)
    cell = ((p_at - 8 * gz + 65) & 63) - 1
    spread = jnp.where(cell <= 8, composite4(z_at, cell), 0.0)
    q_at = iota((64, 128), 0)
    k_at = iota((64, 128), 1)
    picked = jnp.where((q_at == ((8 * (k_at >> 4) + (k_at & 15) + 63) & 63)) & ((k_at & 15) < 10), 1.0, 0.0)
    top_mix = dot3(dot3(spread, top_z[...]), picked)

    for copy in copies_b:
        copy.wait_recv()

    def level1_y(step, carry):
        for u in range(13):
            smooth_y(fext, band_y1, v1, step * 13 + u)
        return carry

    lax.fori_loop(0, 2, level1_y, 0)
    smooth_x(v1, y1, 1, 10, 16)
    y1h, y1l = split(y1[...])
    zs1[:, 0:160] = dot(edge_h, y1h, nt) + dot(edge_h, y1l, nt) + dot(edge_l, y1h, nt)
    zs1[:, 160:256] = jnp.zeros((32, 96), F32)
    copies_z1 = [
        remote(zs1.at[pl.ds(0, 16)], zr1.at[pl.ds(0, 16)], z_send.at[2], z_recv.at[2], left),
        remote(zs1.at[pl.ds(16, 16)], zr1.at[pl.ds(16, 16)], z_send.at[3], z_recv.at[3], right),
    ]
    for copy in copies_z1:
        copy.start()
    level1 = dot(y1h, main_h) + dot(y1h, main_l) + dot(y1l, main_h)

    for copy in copies_t3:
        copy.wait_recv()
    total = rx3[0]
    for o in range(1, nz):
        total = total + rx3[o]
    level1 = level1 + dot3(c_p3[...], dot3(total, top_mix, nt))

    for copy in copies_z0:
        copy.wait_recv()
    tn = ((0,), (0,))
    zh, zl = split(zr0[...])
    potential = out[...].reshape(256, 128) + dot(zh, c_sel[...], tn) + dot(zl, c_sel[...], tn)
    for copy in copies_z1:
        copy.wait_recv()
    zh, zl = split(zr1[...])
    side = dot(zh, c_edge[...], tn) + dot(zl, c_edge[...], tn)
    level1 = level1 + side[0:160]
    lh, ll = split(level1)
    out[...] = (potential + dot(c_pp[...], lh) + dot(c_pp[...], ll)).reshape(16, 16, 128)

    for copy in copies_t1 + copies_a + copies_t2 + copies_b + copies_t3 + copies_z0 + copies_z1:
        copy.wait_send()


def solution(mesh):
    sizes = tuple(mesh.shape[axis] for axis in AXES)
    consts = tables()

    def local(charges, exponents, amplitudes, top_x, top_y, top_z):
        vmem = pl.BlockSpec(memory_space=pltpu.VMEM)
        smem = pl.BlockSpec(memory_space=pltpu.SMEM)
        return pl.pallas_call(
            functools.partial(kernel, sizes),
            out_shape=jax.ShapeDtypeStruct(charges.shape, F32),
            in_specs=[vmem, smem, smem, vmem, vmem, vmem] + [vmem] * len(consts),
            out_specs=vmem,
            scratch_shapes=[
                pltpu.VMEM((32, 32, 128), F32),
                pltpu.VMEM((32, 64, 128), F32),
                pltpu.VMEM((256, 512), F32),
                pltpu.VMEM((26, 32, 128), F32),
                pltpu.VMEM((10, 8, 128), F32),
                pltpu.VMEM((26, 64, 128), F32),
                pltpu.VMEM((160, 512), F32),
                pltpu.VMEM((8, 16, 128), F32),
                pltpu.VMEM((8, 16, 128), F32),
                pltpu.VMEM((8, 16, 128), F32),
                pltpu.VMEM((16, 128), F32),
                pltpu.VMEM((16, 128), F32),
                pltpu.VMEM((16, 128), F32),
                pltpu.VMEM((16, 256), F32),
                pltpu.VMEM((32, 256), F32),
                pltpu.VMEM((16, 256), F32),
                pltpu.VMEM((32, 256), F32),
                pltpu.VMEM((72, 8, 128), F32),
                pltpu.VMEM((8, 8, 128), F32),
                pltpu.SemaphoreType.DMA((8,)),
                pltpu.SemaphoreType.DMA((8,)),
                pltpu.SemaphoreType.DMA((8,)),
                pltpu.SemaphoreType.DMA((8,)),
                pltpu.SemaphoreType.DMA((24,)),
                pltpu.SemaphoreType.DMA((24,)),
                pltpu.SemaphoreType.DMA((4,)),
                pltpu.SemaphoreType.DMA((4,)),
            ],
            compiler_params=pltpu.CompilerParams(
                collective_id=0, has_side_effects=True, vmem_limit_bytes=40 * 2**20
            ),
        )(charges, exponents, amplitudes, top_x, top_y, top_z, *[jnp.asarray(c) for c in consts])

    in_specs = (P("gx", "gy", "gz"), P(), P(), P(), P(), P())
    return jax.shard_map(local, mesh=mesh, in_specs=in_specs, out_specs=P("gx", "gy", "gz"), check_vma=False)
```

```python
import functools

import jax
import jax.numpy as jnp
import numpy as np
from jax import lax
from jax.experimental import pallas as pl
from jax.experimental.pallas import tpu as pltpu
from jax.sharding import PartitionSpec as P

MESH = pl.DeviceIdType.MESH
TERMS = 4
REACH = 8
F32 = jnp.float32
BF16 = jnp.bfloat16
NEAR = [(dx, dy) for dx in (-1, 0, 1) for dy in (-1, 0, 1) if (dx, dy) != (0, 0)]
AXES = ("gx", "gy", "gz")


def spline_np(off):
    off = np.asarray(off)
    return np.where((off == 1) | (off == 2), 0.75, np.where((off == 0) | (off == 3), 0.25, 0.0))


def composite_np(levels):
    box = np.ones(2**levels)
    return np.convolve(np.convolve(box, box), box) / 4.0**levels


def composite_at(levels, fine, cell):
    taps = composite_np(levels)
    off = fine - (cell * 2**levels - (2**levels - 1))
    return np.where((off >= 0) & (off < len(taps)), taps[np.clip(off, 0, len(taps) - 1)], 0.0)


def tables():
    x = np.arange(16)[:, None]
    i = np.arange(10)[None, :]
    px = spline_np(x - 2 * i + 3)
    j = np.arange(16)[None, :]
    py = np.where(j < 10, spline_np(x - 2 * j + 3), 0.0)
    pp = np.einsum("xi,yj->xyij", px, py).reshape(256, 160)
    row = np.arange(128)[:, None]
    lane = np.arange(128)[None, :]
    rt = spline_np(lane - 2 * row + 3)
    m = np.arange(24)[:, None]
    yi = np.arange(32)[None, :]
    ry = np.where(m < 10, spline_np(yi - 2 * m - 5), np.where(m >= 16, spline_np(yi - 2 * m + 23), 0.0))
    ry2 = np.concatenate([ry, ry], axis=1)
    r = np.arange(16)
    a, b = r >> 2, r & 3
    wa = composite_at(4, np.arange(16)[None, :], a[:, None] - 1) * (a < 3)[:, None]
    wb = composite_at(4, np.arange(16)[None, :], b[:, None] - 1) * (b < 3)[:, None]
    w9 = np.einsum("rx,ry->rxy", wa, wb).reshape(16, 256)
    p4 = w9.T
    mm = np.arange(32)[:, None]
    zf = np.arange(128)[None, :]
    cell = np.where(mm < 16, 55 + mm, mm - 17)
    edge = np.where((mm % 16) < 10, spline_np(zf - 2 * cell + 1), 0.0)
    t = np.arange(16)[:, None]
    sel = (zf == np.where(t < 8, 120 + t, t - 8)).astype(np.float64)
    bf = lambda v: np.asarray(v, np.float32).astype(jnp.bfloat16)
    lo = lambda v: np.asarray(v, np.float32) - bf(v).astype(np.float32)
    packed = np.zeros((464, 256), jnp.bfloat16)
    packed[0:256, 0:160] = bf(pp)
    packed[0:256, 160:176] = bf(p4)
    packed[0:256, 176:192] = bf(lo(p4))
    packed[256:384, 0:128] = bf(rt)
    packed[256:384, 128:256] = bf(rt.T)
    packed[384:416, 0:128] = bf(edge)
    packed[384:408, 128:192] = bf(ry2)
    packed[416:432, 0:128] = bf(sel)
    packed[432:448] = bf(w9)
    packed[448:464] = bf(lo(w9))
    return packed


def split(v):
    hi = v.astype(BF16)
    return hi, (v - hi.astype(F32)).astype(BF16)


def dot(a, b, dims=((1,), (0,))):
    return lax.dot_general(a, b, (dims, ((), ())), preferred_element_type=F32)


def dot3(a, b, dims=((1,), (0,))):
    ah, al = split(a)
    bh, bl = split(b)
    return dot(ah, bh, dims) + dot(ah, bl, dims) + dot(al, bh, dims)


def iota(shape, dim):
    return lax.broadcasted_iota(jnp.int32, shape, dim)


def by_term(values, index):
    out = jnp.where(index == 0, values[0], values[1])
    for t in range(2, TERMS):
        out = jnp.where(index == t, values[t], out)
    return out


def composite4(fine, cell):
    off = fine - (cell * 16 - 15)

    def pairs(shift):
        m = jnp.maximum(off + shift, 0).astype(F32)
        return m * (m - 1.0) * 0.5

    return (pairs(2) - 3.0 * pairs(-14) + 3.0 * pairs(-30) - pairs(-46)) * (1.0 / 256.0)


def kernel(
    sizes,
    charges, exps_in, amps_in, top_x_in, top_y_in, top_z_in, table_in,
    out,
    exps, amps, top_x, top_y, top_z, table, load_sem,
    ext, v0, y0, fext, q2, v1, y1,
    rx1, rx2, rx3, tx1, tx2, tx3,
    zs0, zs1, zr0, zr1,
    taps, inv,
    a_send, a_recv, b_send, b_recv, t_send, t_recv, z_send, z_recv,
):
    nx, ny, nz = sizes
    me = [lax.axis_index(axis) for axis in AXES]
    gx, gy, gz = me

    def at(dx, dy, dz):
        return (lax.rem(gx + dx + nx, nx), lax.rem(gy + dy + ny, ny), lax.rem(gz + dz + nz, nz))

    partners = [(dx, dy, 0) for dx, dy in NEAR]
    partners += [(o, 0, 0) for o in range(2, nx - 1)]
    partners += [(0, o, 0) for o in range(2, ny - 1)]
    partners += [(0, 0, o) for o in range(1, nz)]
    barrier = pltpu.get_barrier_semaphore()
    for p in partners:
        pl.semaphore_signal(barrier, inc=1, device_id=at(*p), device_id_type=MESH)

    loads = [
        pltpu.make_async_copy(source, target, load_sem.at[n])
        for n, (source, target) in enumerate(
            [
                (charges, ext.at[pl.ds(8, 16), pl.ds(8, 16), :]),
                (table_in, table),
                (exps_in, exps),
                (amps_in, amps),
                (top_x_in, top_x),
                (top_y_in, top_y),
                (top_z_in, top_z),
            ]
        )
    ]
    for load in loads:
        load.start()
    pl.semaphore_wait(barrier, len(partners))

    def remote(src, dst, send, recv, where):
        return pltpu.make_async_remote_copy(
            src_ref=src, dst_ref=dst, send_sem=send, recv_sem=recv, device_id=at(*where), device_id_type=MESH
        )

    def top_copies(step, src, dst):
        shift = [(1, 0, 0), (0, 1, 0), (0, 0, 1)][step]
        return [
            remote(
                src, dst.at[o], t_send.at[step * 8 + o], t_recv.at[step * 8 + o],
                (shift[0] * o, shift[1] * o, shift[2] * o),
            )
            for o in range(1, sizes[step])
        ]

    source_a = {-1: pl.ds(0, 8), 0: pl.ds(0, 16), 1: pl.ds(8, 8)}
    target_a = {-1: pl.ds(24, 8), 0: pl.ds(8, 16), 1: pl.ds(0, 8)}
    copies_a = [
        remote(
            charges.at[source_a[dx], source_a[dy], :], ext.at[target_a[dx], target_a[dy], :],
            a_send.at[n], a_recv.at[n], (dx, dy, 0),
        )
        for n, (dx, dy) in enumerate(NEAR)
    ]
    for copy in copies_a:
        copy.start()

    for load in loads:
        load.wait()
    own = ext[8:24, 8:24, :]
    c_rt, c_r = table[256:384, 0:128], table[256:384, 128:256]
    c_edge, c_ry, c_sel = table[384:416, 0:128], table[384:408, 128:192], table[416:432, 0:128]

    flat_h, flat_l = split(own.reshape(256, 128))
    w9_h, w9_l = table[432:448, :], table[448:464, :]
    part = dot(w9_h, flat_h) + dot(w9_h, flat_l) + dot(w9_l, flat_h)
    zi = iota((128, 128), 0)
    lane = iota((128, 128), 1)
    slot = lane & 15
    place = jnp.where(((lane >> 4) == gz) & (slot < 10), composite4(zi, slot - 1), 0.0)
    tx1[...] = dot3(part, place)
    rx1[0] = tx1[...]

    copies_t1 = top_copies(0, tx1, rx1)
    for copy in copies_t1:
        copy.start()

    for level in range(2):
        for r in range(TERMS):
            e = jnp.full((8, 128), exps[level, r], F32)
            weights = [jnp.exp(-e * float(k * k)) for k in range(REACH + 1)]
            total = weights[1]
            for k in range(2, REACH + 1):
                total = total + weights[k]
            inverse = 1.0 / (1.0 + 2.0 * total)
            inv[level * TERMS + r] = inverse
            for k in range(REACH + 1):
                taps[(level * TERMS + r) * 9 + k] = weights[k] * inverse * amps[level, r]

    def band(level, term, offset):
        if isinstance(term, int):
            e = exps[level, term]
            scale = inv[level * TERMS + term][0:1, 0:1]
        else:
            e = by_term([exps[level, t] for t in range(TERMS)], term)
            scale = by_term([inv[level * TERMS + t][0:1, 0:1] for t in range(TERMS)], term)
        far = offset.astype(F32)
        return jnp.where(jnp.abs(offset) <= REACH, jnp.exp(-e * (far * far)) * scale, 0.0)

    def tripled(matrix, copy_at):
        hi = matrix.astype(BF16)
        lo = (matrix - hi.astype(F32)).astype(BF16)
        return jnp.where(copy_at == 1, lo.astype(F32), hi.astype(F32)).astype(BF16)

    row = iota((64, 96), 0)
    col = iota((64, 96), 1)
    col32 = col & 31
    band_y0 = tripled(band(0, row >> 4, col32 - 8 - (row & 15)), col >> 5)
    where1 = jnp.where(col32 < 18, col32 - 9, jnp.where(col32 >= 24, col32 - 15, 1000))
    off1 = jnp.where((row & 15) < 10, where1 - ((row & 15) - 1), 1000)
    band_y1 = tripled(band(1, row >> 4, off1), col >> 5)

    def tops(table, own, shape_sizes, first):
        r8 = iota((16, 8), 0)
        p8 = iota((16, 8), 1)
        c8 = iota((8, 128), 0)
        l8 = iota((8, 128), 1)
        rr = iota((16, 128), 0)
        ll = iota((16, 128), 1)
        if first:
            mine, theirs = r8 >> 2, (l8 & 15) >> 2
            same = (rr & 3) == (ll & 3)
        else:
            mine, theirs = r8 & 3, l8 & 3
            same = (rr >> 2) == ((ll & 15) >> 2)
        pick_rows = (p8 == ((own + mine + 7) & 7)).astype(F32)
        pick_cols = (c8 == ((own - (l8 >> 4) + theirs + 15) & 7)).astype(F32)
        whole = dot3(dot3(pick_rows, table), pick_cols)
        valid = ((rr >> 2) < 3) & ((rr & 3) < 3) & (((ll & 15) >> 2) < 3) & ((ll & 3) < 3)
        return jnp.where(same & valid, whole, 0.0)

    zi = iota((128, 128), 0)
    zo = iota((128, 128), 1)
    band_z0 = jnp.concatenate([band(0, r, zi - zo) for r in range(TERMS)], axis=0)
    h_row = iota((16, 128), 0)
    h_lane = iota((16, 128), 1)
    h_out = jnp.where(h_row < 8, h_row - 8, h_row + 120)
    edge_z0 = jnp.concatenate([band(0, r, h_lane - h_out) for r in range(TERMS)], axis=1)
    mix_x = tops(top_x[...], gx, sizes, True)
    mix_y = tops(top_y[...], gy, sizes, False)

    for copy in copies_a:
        copy.wait_recv()

    for i in range(10):
        rx = 0.25 * (ext[2 * i + 5] + ext[2 * i + 8]) + 0.75 * (ext[2 * i + 6] + ext[2 * i + 7])
        hi, lo = split(rx)
        cells = dot(c_ry, jnp.concatenate([hi, lo], axis=0))
        fext[8 + i, 8:24, :] = cells[0:16]
        q2[i] = cells[16:24]

    xs = {-1: pl.ds(10, 8), 0: pl.ds(8, 10), 1: pl.ds(8, 8)}
    xd = {-1: pl.ds(18, 8), 0: pl.ds(8, 10), 1: pl.ds(0, 8)}
    yd = {-1: pl.ds(24, 8), 0: pl.ds(8, 16), 1: pl.ds(0, 8)}
    copies_b = []
    for n, (dx, dy) in enumerate(NEAR):
        if dy == -1:
            src = q2.at[pl.ds(xs[dx].start - 8, xs[dx].size)]
        else:
            src = fext.at[xs[dx], pl.ds(8, 16 if dy == 0 else 8), :]
        copies_b.append(
            remote(src, fext.at[xd[dx], yd[dy], :], b_send.at[n], b_recv.at[n], (dx, dy, 0))
        )
    for copy in copies_b:
        copy.start()

    for n, copy in enumerate(copies_t1):
        copy.wait_recv()
    tx2[...] = dot3(mix_x, rx1[...].reshape(128, 128))
    rx2[0] = tx2[...]
    copies_t2 = top_copies(1, tx2, rx2)
    for copy in copies_t2:
        copy.start()

    g_row = iota((32, 128), 0)
    g_cell = iota((32, 128), 1) - 1
    g_out = jnp.where(g_row < 16, g_row - 9, g_row + 47)
    g_out = jnp.where((g_row & 15) < 10, g_out, 1000)
    mains, edges = [], []
    for r in range(TERMS):
        gh, gl = split(band(1, r, zi - zo))
        ch, cl = split(dot(c_r, gh) + dot(c_r, gl))
        mains.append(dot(ch, c_rt) + dot(cl, c_rt))
        eh, el = split(band(1, r, g_cell - g_out))
        edges.append(dot(eh, c_rt) + dot(el, c_rt))
    main_h, main_l = split(jnp.concatenate(mains, axis=0))
    edge_h, edge_l = split(jnp.concatenate(edges, axis=1))

    p_at = iota((128, 64), 1)
    z_at = iota((128, 64), 0)
    cell = ((p_at - 8 * gz + 65) & 63) - 1
    spread = jnp.where(cell <= 8, composite4(z_at, cell), 0.0)
    q_at = iota((64, 128), 0)
    k_at = iota((64, 128), 1)
    picked = jnp.where((q_at == ((8 * (k_at >> 4) + (k_at & 15) + 63) & 63)) & ((k_at & 15) < 10), 1.0, 0.0)
    top_mix = dot3(dot3(spread, top_z[...]), picked)

    def smooth_y(source, band_y, target, at_x):
        hi, lo = split(source[at_x])
        target[at_x] = dot(band_y, jnp.concatenate([hi, hi, lo], axis=0))

    def level0_y(step, carry):
        for u in range(8):
            smooth_y(ext, band_y0, v0, step * 8 + u)
        return carry

    lax.fori_loop(0, 4, level0_y, 0)

    def smooth_x(source, target, level, count, stride):
        for r in range(TERMS):
            w = [taps[(level * TERMS + r) * 9 + k] for k in range(9)]
            for half in range(2):
                rows = slice(r * 16 + half * 8, r * 16 + half * 8 + 8)
                for x in range(count):
                    acc = w[0] * source[x + 8, rows, :]
                    for k in range(1, 9):
                        acc = acc + w[k] * (source[x + 8 - k, rows, :] + source[x + 8 + k, rows, :])
                    target[x * 16 + half * 8 : x * 16 + half * 8 + 8, r * 128 : r * 128 + 128] = acc

    smooth_x(v0, y0, 0, 16, 16)

    y0h, y0l = split(y0[...])
    eh, el = split(edge_z0)
    nt = ((1,), (1,))
    zs0[...] = dot(eh, y0h, nt) + dot(eh, y0l, nt) + dot(el, y0h, nt)
    left, right = (0, 0, -1), (0, 0, 1)
    copies_z0 = [
        remote(zs0.at[pl.ds(0, 8)], zr0.at[pl.ds(0, 8)], z_send.at[0], z_recv.at[0], left),
        remote(zs0.at[pl.ds(8, 8)], zr0.at[pl.ds(8, 8)], z_send.at[1], z_recv.at[1], right),
    ]
    for copy in copies_z0:
        copy.start()
    bh, bl = split(band_z0)
    out[...] = (dot(y0h, bh) + dot(y0h, bl) + dot(y0l, bh)).reshape(16, 16, 128)

    for copy in copies_t2:
        copy.wait_recv()
    tx3[...] = dot3(mix_y, rx2[...].reshape(128, 128))
    rx3[0] = tx3[...]
    copies_t3 = top_copies(2, tx3, rx3)
    for copy in copies_t3:
        copy.start()

    for copy in copies_b:
        copy.wait_recv()

    def level1_y(step, carry):
        for u in range(13):
            smooth_y(fext, band_y1, v1, step * 13 + u)
        return carry

    lax.fori_loop(0, 2, level1_y, 0)
    smooth_x(v1, y1, 1, 10, 16)
    y1h, y1l = split(y1[...])
    zs1[:, 0:160] = dot(edge_h, y1h, nt) + dot(edge_h, y1l, nt) + dot(edge_l, y1h, nt)
    zs1[:, 160:256] = jnp.zeros((32, 96), F32)
    copies_z1 = [
        remote(zs1.at[pl.ds(0, 16)], zr1.at[pl.ds(0, 16)], z_send.at[2], z_recv.at[2], left),
        remote(zs1.at[pl.ds(16, 16)], zr1.at[pl.ds(16, 16)], z_send.at[3], z_recv.at[3], right),
    ]
    for copy in copies_z1:
        copy.start()
    level1 = dot(y1h, main_h) + dot(y1h, main_l) + dot(y1l, main_h)

    for copy in copies_t3:
        copy.wait_recv()
    total = rx3[0]
    for o in range(1, nz):
        total = total + rx3[o]
    top_h, top_l = split(dot3(total, top_mix, nt))

    for copy in copies_z0:
        copy.wait_recv()
    tn = ((0,), (0,))
    zh, zl = split(zr0[...])
    potential = out[...].reshape(256, 128) + dot(zh, c_sel, tn) + dot(zl, c_sel, tn)
    for copy in copies_z1:
        copy.wait_recv()
    zh, zl = split(zr1[...])
    side = dot(zh, c_edge, tn) + dot(zl, c_edge, tn)
    level1 = level1 + side[0:160]
    lh, ll = split(level1)
    potential = potential + dot(table[0:256, 0:192], jnp.concatenate([lh, top_h, top_h], axis=0))
    potential = potential + dot(table[0:256, 0:176], jnp.concatenate([ll, top_l], axis=0))
    out[...] = potential.reshape(16, 16, 128)

    for copy in copies_t1 + copies_a + copies_t2 + copies_b + copies_t3 + copies_z0 + copies_z1:
        copy.wait_send()


def solution(mesh):
    sizes = tuple(mesh.shape[axis] for axis in AXES)
    packed = tables()

    def local(charges, exponents, amplitudes, top_x, top_y, top_z):
        vmem = pl.BlockSpec(memory_space=pltpu.VMEM)
        hbm = pl.BlockSpec(memory_space=pltpu.HBM)
        return pl.pallas_call(
            functools.partial(kernel, sizes),
            out_shape=jax.ShapeDtypeStruct(charges.shape, F32),
            in_specs=[hbm] * 7,
            out_specs=vmem,
            scratch_shapes=[
                pltpu.SMEM((2, TERMS), F32),
                pltpu.SMEM((2, TERMS), F32),
                pltpu.VMEM(top_x.shape, F32),
                pltpu.VMEM(top_y.shape, F32),
                pltpu.VMEM(top_z.shape, F32),
                pltpu.VMEM(packed.shape, BF16),
                pltpu.SemaphoreType.DMA((7,)),
                pltpu.VMEM((32, 32, 128), F32),
                pltpu.VMEM((32, 64, 128), F32),
                pltpu.VMEM((256, 512), F32),
                pltpu.VMEM((26, 32, 128), F32),
                pltpu.VMEM((10, 8, 128), F32),
                pltpu.VMEM((26, 64, 128), F32),
                pltpu.VMEM((160, 512), F32),
                pltpu.VMEM((8, 16, 128), F32),
                pltpu.VMEM((8, 16, 128), F32),
                pltpu.VMEM((8, 16, 128), F32),
                pltpu.VMEM((16, 128), F32),
                pltpu.VMEM((16, 128), F32),
                pltpu.VMEM((16, 128), F32),
                pltpu.VMEM((16, 256), F32),
                pltpu.VMEM((32, 256), F32),
                pltpu.VMEM((16, 256), F32),
                pltpu.VMEM((32, 256), F32),
                pltpu.VMEM((72, 8, 128), F32),
                pltpu.VMEM((8, 8, 128), F32),
                pltpu.SemaphoreType.DMA((8,)),
                pltpu.SemaphoreType.DMA((8,)),
                pltpu.SemaphoreType.DMA((8,)),
                pltpu.SemaphoreType.DMA((8,)),
                pltpu.SemaphoreType.DMA((24,)),
                pltpu.SemaphoreType.DMA((24,)),
                pltpu.SemaphoreType.DMA((4,)),
                pltpu.SemaphoreType.DMA((4,)),
            ],
            compiler_params=pltpu.CompilerParams(
                collective_id=0, has_side_effects=True, vmem_limit_bytes=40 * 2**20
            ),
        )(*[
            pltpu.with_memory_space_constraint(v, pltpu.HBM)
            for v in (charges, exponents, amplitudes, top_x, top_y, top_z, jnp.asarray(packed))
        ])

    in_specs = (P("gx", "gy", "gz"), P(), P(), P(), P(), P())
    return jax.shard_map(local, mesh=mesh, in_specs=in_specs, out_specs=P("gx", "gy", "gz"), check_vma=False)
```

```python
import functools

import jax
import jax.numpy as jnp
import numpy as np
from jax import lax
from jax.experimental import pallas as pl
from jax.experimental.pallas import tpu as pltpu
from jax.sharding import PartitionSpec as P

MESH = pl.DeviceIdType.MESH
TERMS = 4
REACH = 8
F32 = jnp.float32
BF16 = jnp.bfloat16
NEAR = [(dx, dy) for dx in (-1, 1) for dy in (-1, 1)] + [(-1, 0), (1, 0), (0, -1), (0, 1)]
AXES = ("gx", "gy", "gz")


def spline_np(off):
    off = np.asarray(off)
    return np.where((off == 1) | (off == 2), 0.75, np.where((off == 0) | (off == 3), 0.25, 0.0))


def composite_np(levels):
    box = np.ones(2**levels)
    return np.convolve(np.convolve(box, box), box) / 4.0**levels


def composite_at(levels, fine, cell):
    taps = composite_np(levels)
    off = fine - (cell * 2**levels - (2**levels - 1))
    return np.where((off >= 0) & (off < len(taps)), taps[np.clip(off, 0, len(taps) - 1)], 0.0)


def tables():
    x = np.arange(16)[:, None]
    i = np.arange(10)[None, :]
    px = spline_np(x - 2 * i + 3)
    j = np.arange(16)[None, :]
    py = np.where(j < 10, spline_np(x - 2 * j + 3), 0.0)
    pp = np.einsum("xi,yj->xyij", px, py).reshape(256, 160)
    row = np.arange(128)[:, None]
    lane = np.arange(128)[None, :]
    rt = spline_np(lane - 2 * row + 3)
    m = np.arange(24)[:, None]
    yi = np.arange(32)[None, :]
    ry = np.where(m < 10, spline_np(yi - 2 * m - 5), np.where(m >= 16, spline_np(yi - 2 * m + 23), 0.0))
    ry2 = np.concatenate([ry, ry], axis=1)
    r = np.arange(16)
    a, b = r >> 2, r & 3
    wa = composite_at(4, np.arange(16)[None, :], a[:, None] - 1) * (a < 3)[:, None]
    wb = composite_at(4, np.arange(16)[None, :], b[:, None] - 1) * (b < 3)[:, None]
    w9 = np.einsum("rx,ry->rxy", wa, wb).reshape(16, 256)
    p4 = w9.T
    mm = np.arange(32)[:, None]
    zf = np.arange(128)[None, :]
    cell = np.where(mm < 16, 55 + mm, mm - 17)
    edge = np.where((mm % 16) < 10, spline_np(zf - 2 * cell + 1), 0.0)
    t = np.arange(16)[:, None]
    sel = (zf == np.where(t < 8, 120 + t, t - 8)).astype(np.float64)
    bf = lambda v: np.asarray(v, np.float32).astype(jnp.bfloat16)
    lo = lambda v: np.asarray(v, np.float32) - bf(v).astype(np.float32)
    lanes = np.arange(128)
    lane_a, lane_b, lane_c = lanes // 30, lanes // 10 % 3, lanes % 10
    place = composite_at(4, np.arange(128)[:, None], lane_c[None, :] - 1) * (lanes < 90)
    own_row = (np.arange(16)[:, None] == (lane_a * 4 + lane_b)[None, :]) & (lanes < 90)
    packed = np.zeros((592, 256), jnp.bfloat16)
    packed[464:592, 0:128] = bf(place)
    packed[416:432, 128:256] = bf(own_row)
    packed[0:256, 0:160] = bf(pp)
    packed[0:256, 160:176] = bf(p4)
    packed[0:256, 176:192] = bf(lo(p4))
    packed[0:256, 192:208] = bf(p4)
    packed[256:384, 0:128] = bf(rt)
    packed[256:384, 128:256] = bf(rt.T)
    packed[384:416, 0:128] = bf(edge)
    packed[384:408, 128:192] = bf(ry2)
    packed[416:432, 0:128] = bf(sel)
    packed[432:448] = bf(w9)
    packed[448:464] = bf(lo(w9))
    return packed


def split(v):
    hi = v.astype(BF16)
    return hi, (v - hi.astype(F32)).astype(BF16)


def dot(a, b, dims=((1,), (0,))):
    return lax.dot_general(a, b, (dims, ((), ())), preferred_element_type=F32)


def dot3(a, b, dims=((1,), (0,))):
    ah, al = split(a)
    bh, bl = split(b)
    return dot(ah, bh, dims) + dot(ah, bl, dims) + dot(al, bh, dims)


def iota(shape, dim):
    return lax.broadcasted_iota(jnp.int32, shape, dim)


def by_term(values, index):
    out = jnp.where(index == 0, values[0], values[1])
    for t in range(2, TERMS):
        out = jnp.where(index == t, values[t], out)
    return out


def composite4(fine, cell):
    off = fine - (cell * 16 - 15)

    def pairs(shift):
        m = jnp.maximum(off + shift, 0).astype(F32)
        return m * (m - 1.0) * 0.5

    return (pairs(2) - 3.0 * pairs(-14) + 3.0 * pairs(-30) - pairs(-46)) * (1.0 / 256.0)


def kernel(
    sizes,
    charges, exps_in, amps_in, top_x_in, top_y_in, top_z_in, table_in,
    out,
    exps, amps, top_x, top_y, top_z, table, load_sem,
    ext, v0, y0, fext, q2, v1, y1,
    rx1, rx2, rx3,
    zs0, zs1, zr0, zr1,
    taps, inv,
    a_send, a_recv, b_send, b_recv, t_send, t_recv, z_send, z_recv,
):
    nx, ny, nz = sizes
    me = [lax.axis_index(axis) for axis in AXES]
    gx, gy, gz = me

    def at(dx, dy, dz):
        return (lax.rem(gx + dx + nx, nx), lax.rem(gy + dy + ny, ny), lax.rem(gz + dz + nz, nz))

    partners = [(dx, dy, 0) for dx, dy in NEAR]
    partners += [(o, 0, 0) for o in range(2, nx - 1)]
    partners += [(0, o, 0) for o in range(2, ny - 1)]
    partners += [(0, 0, o) for o in range(1, nz)]
    barrier = pltpu.get_barrier_semaphore()
    for p in partners:
        pl.semaphore_signal(barrier, inc=1, device_id=at(*p), device_id_type=MESH)

    loads = [
        pltpu.make_async_copy(source, target, load_sem.at[n])
        for n, (source, target) in enumerate(
            [
                (charges, ext.at[pl.ds(8, 16), pl.ds(8, 16), :]),
                (table_in, table),
                (exps_in, exps),
                (amps_in, amps),
                (top_x_in, top_x),
                (top_y_in, top_y),
                (top_z_in, top_z),
            ]
        )
    ]
    for load in loads:
        load.start()

    def remote(src, dst, send, recv, where):
        return pltpu.make_async_remote_copy(
            src_ref=src, dst_ref=dst, send_sem=send, recv_sem=recv, device_id=at(*where), device_id_type=MESH
        )

    def top_copies(step, src, dst):
        shift = [(1, 0, 0), (0, 1, 0), (0, 0, 1)][step]
        return [
            remote(
                src, dst.at[o], t_send.at[step * 8 + o], t_recv.at[step * 8 + o],
                (shift[0] * o, shift[1] * o, shift[2] * o),
            )
            for o in range(1, sizes[step])
        ]

    for load in loads[:2]:
        load.wait()
    own = ext[8:24, 8:24, :]
    c_rt, c_r = table[256:384, 0:128], table[256:384, 128:256]
    c_edge, c_ry, c_sel = table[384:416, 0:128], table[384:408, 128:192], table[416:432, 0:128]

    flat_h, flat_l = split(own.reshape(256, 128))
    w9_h, w9_l = table[432:448, :], table[448:464, :]
    part = dot(w9_h, flat_h) + dot(w9_h, flat_l) + dot(w9_l, flat_h)
    part_h, part_l = split(part)
    place = table[464:592, 0:128]
    placed = (dot(part_h, place) + dot(part_l, place)) * table[416:432, 128:256].astype(F32)
    rx1[0] = jnp.sum(placed, axis=0, keepdims=True)

    pl.semaphore_wait(barrier, len(partners))
    source_a = {-1: pl.ds(0, 8), 0: pl.ds(0, 16), 1: pl.ds(8, 8)}
    target_a = {-1: pl.ds(24, 8), 0: pl.ds(8, 16), 1: pl.ds(0, 8)}
    copies_a = [
        remote(
            charges.at[source_a[dx], source_a[dy], :], ext.at[target_a[dx], target_a[dy], :],
            a_send.at[n], a_recv.at[n], (dx, dy, 0),
        )
        for n, (dx, dy) in enumerate(NEAR)
    ]
    for copy in copies_a:
        copy.start()

    copies_t1 = top_copies(0, rx1.at[0], rx1)
    for copy in copies_t1:
        copy.start()

    for load in loads[2:]:
        load.wait()

    for level in range(2):
        for r in range(TERMS):
            e = jnp.full((8, 128), exps[level, r], F32)
            weights = [jnp.exp(-e * float(k * k)) for k in range(REACH + 1)]
            total = weights[1]
            for k in range(2, REACH + 1):
                total = total + weights[k]
            inverse = 1.0 / (1.0 + 2.0 * total)
            inv[level * TERMS + r] = inverse
            for k in range(REACH + 1):
                taps[(level * TERMS + r) * 9 + k] = weights[k] * inverse * amps[level, r]

    def band(level, term, offset):
        if isinstance(term, int):
            e = exps[level, term]
            scale = inv[level * TERMS + term][0:1, 0:1]
        else:
            e = by_term([exps[level, t] for t in range(TERMS)], term)
            scale = by_term([inv[level * TERMS + t][0:1, 0:1] for t in range(TERMS)], term)
        far = offset.astype(F32)
        return jnp.where(jnp.abs(offset) <= REACH, jnp.exp(-e * (far * far)) * scale, 0.0)

    def tripled(matrix, copy_at):
        hi = matrix.astype(BF16)
        lo = (matrix - hi.astype(F32)).astype(BF16)
        return jnp.where(copy_at == 1, lo.astype(F32), hi.astype(F32)).astype(BF16)

    row = iota((64, 96), 0)
    col = iota((64, 96), 1)
    col32 = col & 31
    band_y0 = tripled(band(0, row >> 4, col32 - 8 - (row & 15)), col >> 5)
    where1 = jnp.where(col32 < 18, col32 - 9, jnp.where(col32 >= 24, col32 - 15, 1000))
    off1 = jnp.where((row & 15) < 10, where1 - ((row & 15) - 1), 1000)
    band_y1 = tripled(band(1, row >> 4, off1), col >> 5)

    zi = iota((128, 128), 0)
    zo = iota((128, 128), 1)
    band_z0 = jnp.concatenate([band(0, r, zi - zo) for r in range(TERMS)], axis=0)
    h_row = iota((16, 128), 0)
    h_lane = iota((16, 128), 1)
    h_out = jnp.where(h_row < 8, h_row - 8, h_row + 120)
    edge_z0 = jnp.concatenate([band(0, r, h_lane - h_out) for r in range(TERMS)], axis=1)
    slot_at = iota((8, 128), 0)
    lane_at = iota((8, 128), 1)
    tens = (lane_at * 205) >> 11
    lane_a = (tens * 11) >> 5
    lane_b = tens - 3 * lane_a

    def top_weights(kernel_rows, own_at, lane_cell, extent):
        source = (own_at - slot_at + lane_cell + extent - 1) & (extent - 1)
        found = []
        for shift in range(3):
            row_at = lax.rem(own_at + shift + extent - 1, extent)
            weights = jnp.zeros((8, 128), F32)
            for q in range(extent):
                weights = jnp.where(source == q, kernel_rows[row_at, q], weights)
            found.append(weights)
        return found

    weights_x = top_weights(top_x, gx, lane_a, nx)
    weights_y = top_weights(top_y, gy, lane_b, ny)

    l16 = iota((16, 128), 1)
    r16 = iota((16, 128), 0)
    within = l16 - 30 * (r16 >> 2)
    keep_top = (within >= 0) & (within < 10) & (r16 < 12) & ((r16 & 3) < 3)
    from_lane = iota((128, 128), 0)
    from_lane = from_lane - 30 * ((((from_lane * 205) >> 11) * 11) >> 5)
    slot_z = jnp.where((from_lane < 10) & (iota((128, 128), 1) == 16 * gz + from_lane), 1.0, 0.0).astype(BF16)

    def contracted(received, weights, step):
        slots = received[...].reshape(8, 128)
        sums = [jnp.sum(slots * w, axis=0, keepdims=True) for w in weights]
        rows = jnp.where(slot_at == 0, sums[0], jnp.where(slot_at == 1, sums[1], sums[2]))
        return rows + pltpu.roll(rows, 128 - step, 1) + pltpu.roll(rows, 128 - 2 * step, 1)

    for copy in copies_a:
        copy.wait_recv()

    for i in range(10):
        rx = 0.25 * (ext[2 * i + 5] + ext[2 * i + 8]) + 0.75 * (ext[2 * i + 6] + ext[2 * i + 7])
        hi, lo = split(rx)
        cells = dot(c_ry, jnp.concatenate([hi, lo], axis=0))
        fext[8 + i, 8:24, :] = cells[0:16]
        q2[i] = cells[16:24]

    xs = {-1: pl.ds(10, 8), 0: pl.ds(8, 10), 1: pl.ds(8, 8)}
    xd = {-1: pl.ds(18, 8), 0: pl.ds(8, 10), 1: pl.ds(0, 8)}
    yd = {-1: pl.ds(24, 8), 0: pl.ds(8, 16), 1: pl.ds(0, 8)}
    copies_b = []
    for n, (dx, dy) in enumerate(NEAR):
        if dy == -1:
            src = q2.at[pl.ds(xs[dx].start - 8, xs[dx].size)]
        else:
            src = fext.at[xs[dx], pl.ds(8, 16 if dy == 0 else 8), :]
        copies_b.append(
            remote(src, fext.at[xd[dx], yd[dy], :], b_send.at[n], b_recv.at[n], (dx, dy, 0))
        )
    for copy in copies_b:
        copy.start()

    for n, copy in enumerate(copies_t1):
        copy.wait_recv()
    folded = contracted(rx1, weights_x, 30)
    spread_x = jnp.where(slot_at == 0, folded, jnp.where(slot_at == 1, pltpu.roll(folded, 30, 1), pltpu.roll(folded, 60, 1)))
    rx2[0] = jnp.sum(jnp.where(lane_a == slot_at, spread_x, 0.0), axis=0, keepdims=True)
    copies_t2 = top_copies(1, rx2.at[0], rx2)
    for copy in copies_t2:
        copy.start()

    g_row = iota((32, 128), 0)
    g_cell = iota((32, 128), 1) - 1
    g_out = jnp.where(g_row < 16, g_row - 9, g_row + 47)
    g_out = jnp.where((g_row & 15) < 10, g_out, 1000)
    mains, edges = [], []
    for r in range(TERMS):
        gh, gl = split(band(1, r, zi - zo))
        ch, cl = split(dot(c_r, gh) + dot(c_r, gl))
        mains.append(dot(ch, c_rt) + dot(cl, c_rt))
        eh, el = split(band(1, r, g_cell - g_out))
        edges.append(dot(eh, c_rt) + dot(el, c_rt))
    main_h, main_l = split(jnp.concatenate(mains, axis=0))
    edge_h, edge_l = split(jnp.concatenate(edges, axis=1))

    p_at = iota((128, 64), 1)
    z_at = iota((128, 64), 0)
    cell = ((p_at - 8 * gz + 65) & 63) - 1
    spread = jnp.where(cell <= 8, composite4(z_at, cell), 0.0)
    q_at = iota((64, 128), 0)
    k_at = iota((64, 128), 1)
    picked = jnp.where((q_at == ((8 * (k_at >> 4) + (k_at & 15) + 63) & 63)) & ((k_at & 15) < 10), 1.0, 0.0)
    top_mix = dot3(dot3(spread, top_z[...]), picked)

    def smooth_y(source, band_y, target, at_x):
        hi, lo = split(source[at_x])
        target[at_x] = dot(band_y, jnp.concatenate([hi, hi, lo], axis=0))

    def level0_y(step, carry):
        for u in range(8):
            smooth_y(ext, band_y0, v0, step * 8 + u)
        return carry

    lax.fori_loop(0, 4, level0_y, 0)

    def smooth_x(source, target, level, count, stride):
        for r in range(TERMS):
            w = [taps[(level * TERMS + r) * 9 + k] for k in range(9)]
            for half in range(2):
                rows = slice(r * 16 + half * 8, r * 16 + half * 8 + 8)
                for x in range(count):
                    acc = w[0] * source[x + 8, rows, :]
                    for k in range(1, 9):
                        acc = acc + w[k] * (source[x + 8 - k, rows, :] + source[x + 8 + k, rows, :])
                    target[x * 16 + half * 8 : x * 16 + half * 8 + 8, r * 128 : r * 128 + 128] = acc

    smooth_x(v0, y0, 0, 16, 16)

    y0h, y0l = split(y0[...])
    eh, el = split(edge_z0)
    nt = ((1,), (1,))
    zs0[...] = dot(eh, y0h, nt) + dot(eh, y0l, nt) + dot(el, y0h, nt)
    left, right = (0, 0, -1), (0, 0, 1)
    copies_z0 = [
        remote(zs0.at[pl.ds(0, 8)], zr0.at[pl.ds(0, 8)], z_send.at[0], z_recv.at[0], left),
        remote(zs0.at[pl.ds(8, 8)], zr0.at[pl.ds(8, 8)], z_send.at[1], z_recv.at[1], right),
    ]
    for copy in copies_z0:
        copy.start()
    bh, bl = split(band_z0)
    out[...] = (dot(y0h, bh) + dot(y0h, bl) + dot(y0l, bh)).reshape(16, 16, 128)

    for copy in copies_t2:
        copy.wait_recv()
    folded = contracted(rx2, weights_y, 10)
    r16 = iota((16, 128), 0)
    wide = jnp.where((r16 & 3) == 0, folded[0:1], jnp.where((r16 & 3) == 1, folded[1:2], folded[2:3]))
    wide = jnp.where(keep_top, wide, 0.0)
    wide_h, wide_l = split(wide)
    rx3[0] = dot(wide_h, slot_z) + dot(wide_l, slot_z)
    copies_t3 = top_copies(2, rx3.at[0], rx3)
    for copy in copies_t3:
        copy.start()

    for copy in copies_b:
        copy.wait_recv()

    def level1_y(step, carry):
        for u in range(13):
            smooth_y(fext, band_y1, v1, step * 13 + u)
        return carry

    lax.fori_loop(0, 2, level1_y, 0)
    smooth_x(v1, y1, 1, 10, 16)
    y1h, y1l = split(y1[...])
    zs1[:, 0:160] = dot(edge_h, y1h, nt) + dot(edge_h, y1l, nt) + dot(edge_l, y1h, nt)
    zs1[:, 160:256] = jnp.zeros((32, 96), F32)
    copies_z1 = [
        remote(zs1.at[pl.ds(0, 16)], zr1.at[pl.ds(0, 16)], z_send.at[2], z_recv.at[2], left),
        remote(zs1.at[pl.ds(16, 16)], zr1.at[pl.ds(16, 16)], z_send.at[3], z_recv.at[3], right),
    ]
    for copy in copies_z1:
        copy.start()
    level1 = dot(y1h, main_h) + dot(y1h, main_l) + dot(y1l, main_h)

    lh, ll = split(level1)
    from_cells = table[0:256, 0:160]
    potential = out[...].reshape(256, 128) + dot(from_cells, lh) + dot(from_cells, ll)

    for copy in copies_t3:
        copy.wait_recv()
    total = rx3[0]
    for o in range(1, nz):
        total = total + rx3[o]
    top_h, top_l = split(dot3(total, top_mix, nt))
    potential = potential + dot(table[0:256, 160:208], jnp.concatenate([top_h, top_h, top_l], axis=0))

    for copy in copies_z0:
        copy.wait_recv()
    tn = ((0,), (0,))
    zh, zl = split(zr0[...])
    out[...] = (potential + dot(zh, c_sel, tn) + dot(zl, c_sel, tn)).reshape(16, 16, 128)

    for copy in copies_z1:
        copy.wait_recv()
    zh, zl = split(zr1[...])
    side = dot(zh, c_edge, tn) + dot(zl, c_edge, tn)
    lh, ll = split(side[0:160])
    out[...] = out[...] + (dot(from_cells, lh) + dot(from_cells, ll)).reshape(16, 16, 128)

    for copy in copies_t1 + copies_a + copies_t2 + copies_b + copies_t3 + copies_z0 + copies_z1:
        copy.wait_send()


def solution(mesh):
    sizes = tuple(mesh.shape[axis] for axis in AXES)
    packed = tables()

    def local(charges, exponents, amplitudes, top_x, top_y, top_z):
        vmem = pl.BlockSpec(memory_space=pltpu.VMEM)
        hbm = pl.BlockSpec(memory_space=pltpu.HBM)
        return pl.pallas_call(
            functools.partial(kernel, sizes),
            out_shape=jax.ShapeDtypeStruct(charges.shape, F32),
            in_specs=[hbm] * 7,
            out_specs=vmem,
            scratch_shapes=[
                pltpu.SMEM((2, TERMS), F32),
                pltpu.SMEM((2, TERMS), F32),
                pltpu.SMEM(top_x.shape, F32),
                pltpu.SMEM(top_y.shape, F32),
                pltpu.VMEM(top_z.shape, F32),
                pltpu.VMEM(packed.shape, BF16),
                pltpu.SemaphoreType.DMA((7,)),
                pltpu.VMEM((32, 32, 128), F32),
                pltpu.VMEM((32, 64, 128), F32),
                pltpu.VMEM((256, 512), F32),
                pltpu.VMEM((26, 32, 128), F32),
                pltpu.VMEM((10, 8, 128), F32),
                pltpu.VMEM((26, 64, 128), F32),
                pltpu.VMEM((160, 512), F32),
                pltpu.VMEM((8, 1, 128), F32),
                pltpu.VMEM((8, 1, 128), F32),
                pltpu.VMEM((8, 16, 128), F32),
                pltpu.VMEM((16, 256), F32),
                pltpu.VMEM((32, 256), F32),
                pltpu.VMEM((16, 256), F32),
                pltpu.VMEM((32, 256), F32),
                pltpu.VMEM((72, 8, 128), F32),
                pltpu.VMEM((8, 8, 128), F32),
                pltpu.SemaphoreType.DMA((8,)),
                pltpu.SemaphoreType.DMA((8,)),
                pltpu.SemaphoreType.DMA((8,)),
                pltpu.SemaphoreType.DMA((8,)),
                pltpu.SemaphoreType.DMA((24,)),
                pltpu.SemaphoreType.DMA((24,)),
                pltpu.SemaphoreType.DMA((4,)),
                pltpu.SemaphoreType.DMA((4,)),
            ],
            compiler_params=pltpu.CompilerParams(
                collective_id=0, has_side_effects=True, vmem_limit_bytes=40 * 2**20
            ),
        )(*[
            pltpu.with_memory_space_constraint(v, pltpu.HBM)
            for v in (charges, exponents, amplitudes, top_x, top_y, top_z, jnp.asarray(packed))
        ])

    in_specs = (P("gx", "gy", "gz"), P(), P(), P(), P(), P())
    return jax.shard_map(local, mesh=mesh, in_specs=in_specs, out_specs=P("gx", "gy", "gz"), check_vma=False)
```

```python
import functools

import jax
import jax.numpy as jnp
import numpy as np
from jax import lax
from jax.experimental import pallas as pl
from jax.experimental.pallas import tpu as pltpu
from jax.sharding import PartitionSpec as P

MESH = pl.DeviceIdType.MESH
TERMS = 4
REACH = 8
F32 = jnp.float32
BF16 = jnp.bfloat16
NEAR = [(dx, dy) for dx in (-1, 1) for dy in (-1, 1)] + [(-1, 0), (1, 0), (0, -1), (0, 1)]
AXES = ("gx", "gy", "gz")


def spline_np(off):
    off = np.asarray(off)
    return np.where((off == 1) | (off == 2), 0.75, np.where((off == 0) | (off == 3), 0.25, 0.0))


def composite_np(levels):
    box = np.ones(2**levels)
    return np.convolve(np.convolve(box, box), box) / 4.0**levels


def composite_at(levels, fine, cell):
    taps = composite_np(levels)
    off = fine - (cell * 2**levels - (2**levels - 1))
    return np.where((off >= 0) & (off < len(taps)), taps[np.clip(off, 0, len(taps) - 1)], 0.0)


def tables():
    x = np.arange(16)[:, None]
    i = np.arange(10)[None, :]
    px = spline_np(x - 2 * i + 3)
    j = np.arange(16)[None, :]
    py = np.where(j < 10, spline_np(x - 2 * j + 3), 0.0)
    pp = np.einsum("xi,yj->xyij", px, py).reshape(256, 160)
    row = np.arange(128)[:, None]
    lane = np.arange(128)[None, :]
    rt = spline_np(lane - 2 * row + 3)
    m = np.arange(24)[:, None]
    yi = np.arange(32)[None, :]
    ry = np.where(m < 10, spline_np(yi - 2 * m - 5), np.where(m >= 16, spline_np(yi - 2 * m + 23), 0.0))
    ry2 = np.concatenate([ry, ry], axis=1)
    r = np.arange(16)
    a, b = r >> 2, r & 3
    wa = composite_at(4, np.arange(16)[None, :], a[:, None] - 1) * (a < 3)[:, None]
    wb = composite_at(4, np.arange(16)[None, :], b[:, None] - 1) * (b < 3)[:, None]
    w9 = np.einsum("rx,ry->rxy", wa, wb).reshape(16, 256)
    p4 = w9.T
    mm = np.arange(32)[:, None]
    zf = np.arange(128)[None, :]
    cell = np.where(mm < 16, 55 + mm, mm - 17)
    edge = np.where((mm % 16) < 10, spline_np(zf - 2 * cell + 1), 0.0)
    t = np.arange(16)[:, None]
    sel = (zf == np.where(t < 8, 120 + t, t - 8)).astype(np.float64)
    bf = lambda v: np.asarray(v, np.float32).astype(jnp.bfloat16)
    lo = lambda v: np.asarray(v, np.float32) - bf(v).astype(np.float32)
    lanes = np.arange(128)
    lane_a, lane_b, lane_c = lanes // 30, lanes // 10 % 3, lanes % 10
    place = composite_at(4, np.arange(128)[:, None], lane_c[None, :] - 1) * (lanes < 90)
    own_row = (np.arange(16)[:, None] == (lane_a * 4 + lane_b)[None, :]) & (lanes < 90)
    packed = np.zeros((592, 256), jnp.bfloat16)
    packed[464:592, 0:128] = bf(place)
    packed[416:432, 128:256] = bf(own_row)
    packed[0:256, 0:160] = bf(pp)
    packed[0:256, 160:176] = bf(p4)
    packed[0:256, 176:192] = bf(lo(p4))
    packed[0:256, 192:208] = bf(p4)
    packed[256:384, 0:128] = bf(rt)
    packed[256:384, 128:256] = bf(rt.T)
    packed[384:416, 0:128] = bf(edge)
    packed[384:408, 128:192] = bf(ry2)
    packed[416:432, 0:128] = bf(sel)
    packed[432:448] = bf(w9)
    packed[448:464] = bf(lo(w9))
    return packed


def offsets(count, odd_far=False):
    ring = lambda o: min(o, count - o)
    return sorted(range(1, count), key=lambda o: (-(o % 2) if odd_far else 0, -ring(o)))


def split(v):
    hi = v.astype(BF16)
    return hi, (v - hi.astype(F32)).astype(BF16)


def dot(a, b, dims=((1,), (0,))):
    return lax.dot_general(a, b, (dims, ((), ())), preferred_element_type=F32)


def dot3(a, b, dims=((1,), (0,))):
    ah, al = split(a)
    bh, bl = split(b)
    return dot(ah, bh, dims) + dot(ah, bl, dims) + dot(al, bh, dims)


def iota(shape, dim):
    return lax.broadcasted_iota(jnp.int32, shape, dim)


def by_term(values, index):
    out = jnp.where(index == 0, values[0], values[1])
    for t in range(2, TERMS):
        out = jnp.where(index == t, values[t], out)
    return out


def composite4(fine, cell):
    off = fine - (cell * 16 - 15)

    def pairs(shift):
        m = jnp.maximum(off + shift, 0).astype(F32)
        return m * (m - 1.0) * 0.5

    return (pairs(2) - 3.0 * pairs(-14) + 3.0 * pairs(-30) - pairs(-46)) * (1.0 / 256.0)


def kernel(
    sizes,
    charges, exps_in, amps_in, top_x_in, top_y_in, top_z_in, table_in,
    out,
    exps, amps, top_x, top_y, top_z, table, load_sem,
    ext, v0, y0, fext, q2, q3, edge_rows, v1, y1,
    rx1, rx2, rx3,
    zs0, zs1, zr0, zr1,
    taps, inv,
    a_send, a_recv, b_send, b_recv, t_send, t_recv, z_send, z_recv,
):
    nx, ny, nz = sizes
    me = [lax.axis_index(axis) for axis in AXES]
    gx, gy, gz = me

    def at(dx, dy, dz):
        return (lax.rem(gx + dx + nx, nx), lax.rem(gy + dy + ny, ny), lax.rem(gz + dz + nz, nz))

    partners = [(0, 0, o) for o in offsets(nz, True)]
    partners += [(o, 0, 0) for o in offsets(nx) if 1 < o < nx - 1]
    partners += [(0, o, 0) for o in offsets(ny) if 1 < o < ny - 1]
    partners += [(dx, dy, 0) for dx, dy in NEAR]
    barrier = pltpu.get_barrier_semaphore()
    for p in partners:
        pl.semaphore_signal(barrier, inc=1, device_id=at(*p), device_id_type=MESH)

    loads = [
        pltpu.make_async_copy(source, target, load_sem.at[n])
        for n, (source, target) in enumerate(
            [
                (charges, ext.at[pl.ds(8, 16), pl.ds(8, 16), :]),
                (table_in, table),
                (exps_in, exps),
                (amps_in, amps),
                (top_x_in, top_x),
                (top_y_in, top_y),
                (top_z_in, top_z),
            ]
        )
    ]
    for load in loads:
        load.start()

    def remote(src, dst, send, recv, where):
        return pltpu.make_async_remote_copy(
            src_ref=src, dst_ref=dst, send_sem=send, recv_sem=recv, device_id=at(*where), device_id_type=MESH
        )

    def top_copies(step, src, dst):
        shift = [(1, 0, 0), (0, 1, 0), (0, 0, 1)][step]
        return [
            remote(
                src, dst.at[o], t_send.at[step * 8 + o], t_recv.at[step * 8 + o],
                (shift[0] * o, shift[1] * o, shift[2] * o),
            )
            for o in offsets(sizes[step], step == 2)
        ]

    zs1[...] = jnp.zeros_like(zs1)
    edge_rows[:, 16:24, :] = jnp.zeros((2, 8, 128), F32)
    for load in loads[:2]:
        load.wait()
    own = ext[8:24, 8:24, :]
    c_rt, c_r = table[256:384, 0:128], table[256:384, 128:256]
    c_edge, c_ry, c_sel = table[384:416, 0:128], table[384:408, 128:192], table[416:432, 0:128]

    flat_h, flat_l = split(own.reshape(256, 128))
    w9_h, w9_l = table[432:448, :], table[448:464, :]
    part = dot(w9_h, flat_h) + dot(w9_h, flat_l) + dot(w9_l, flat_h)
    part_h, part_l = split(part)
    place = table[464:592, 0:128]
    placed = (dot(part_h, place) + dot(part_l, place)) * table[416:432, 128:256].astype(F32)
    rx1[0] = jnp.sum(placed, axis=0, keepdims=True)

    pl.semaphore_wait(barrier, len(partners))
    source_x = {-1: [(0, 3), (3, 5)], 0: [(0, 16)], 1: [(13, 3), (8, 5)]}
    target_x = {-1: [24, 27], 0: [8], 1: [5, 0]}
    source_y = {-1: (0, 8), 0: (0, 16), 1: (8, 8)}
    target_y = {-1: 24, 0: 8, 1: 0}

    def halo_copies(part):
        found = []
        for n, (dx, dy) in enumerate(NEAR):
            if part < len(source_x[dx]):
                start, size = source_x[dx][part]
                start_y, size_y = source_y[dy]
                found.append(
                    remote(
                        charges.at[pl.ds(start, size), pl.ds(start_y, size_y), :],
                        ext.at[pl.ds(target_x[dx][part], size), pl.ds(target_y[dy], size_y), :],
                        a_send.at[part * 8 + n], a_recv.at[part * 8 + n], (dx, dy, 0),
                    )
                )
        return found

    copies_t1 = top_copies(0, rx1.at[0], rx1)
    for copy in copies_t1:
        copy.start()
    copies_a, copies_far = halo_copies(0), halo_copies(1)
    for copy in copies_a:
        copy.start()
    for copy in copies_far:
        copy.start()

    for load in loads[2:]:
        load.wait()

    for level in range(2):
        for r in range(TERMS):
            e = jnp.full((8, 128), exps[level, r], F32)
            weights = [jnp.exp(-e * float(k * k)) for k in range(REACH + 1)]
            total = weights[1]
            for k in range(2, REACH + 1):
                total = total + weights[k]
            inverse = 1.0 / (1.0 + 2.0 * total)
            inv[level * TERMS + r] = inverse
            for k in range(REACH + 1):
                taps[(level * TERMS + r) * 9 + k] = weights[k] * inverse * amps[level, r]

    def band(level, term, offset):
        if isinstance(term, int):
            e = exps[level, term]
            scale = inv[level * TERMS + term][0:1, 0:1]
        else:
            e = by_term([exps[level, t] for t in range(TERMS)], term)
            scale = by_term([inv[level * TERMS + t][0:1, 0:1] for t in range(TERMS)], term)
        far = offset.astype(F32)
        return jnp.where(jnp.abs(offset) <= REACH, jnp.exp(-e * (far * far)) * scale, 0.0)

    def tripled(matrix, copy_at):
        hi = matrix.astype(BF16)
        lo = (matrix - hi.astype(F32)).astype(BF16)
        return jnp.where(copy_at == 1, lo.astype(F32), hi.astype(F32)).astype(BF16)

    row = iota((64, 96), 0)
    col = iota((64, 96), 1)
    col32 = col & 31
    band_y0 = tripled(band(0, row >> 4, col32 - 8 - (row & 15)), col >> 5)
    where1 = jnp.where(col32 < 18, col32 - 9, jnp.where(col32 >= 24, col32 - 15, 1000))
    off1 = jnp.where((row & 15) < 10, where1 - ((row & 15) - 1), 1000)
    band_y1 = tripled(band(1, row >> 4, off1), col >> 5)

    zi = iota((128, 128), 0)
    zo = iota((128, 128), 1)
    band_z0 = jnp.concatenate([band(0, r, zi - zo) for r in range(TERMS)], axis=0)
    h_row = iota((16, 128), 0)
    h_lane = iota((16, 128), 1)
    h_out = jnp.where(h_row < 8, h_row - 8, h_row + 120)
    edge_z0 = jnp.concatenate([band(0, r, h_lane - h_out) for r in range(TERMS)], axis=1)
    slot_at = iota((8, 128), 0)
    lane_at = iota((8, 128), 1)
    tens = (lane_at * 205) >> 11
    lane_a = (tens * 11) >> 5
    lane_b = tens - 3 * lane_a

    def top_weights(kernel_rows, own_at, lane_cell, extent):
        source = (own_at - slot_at + lane_cell + extent - 1) & (extent - 1)
        found = []
        for shift in range(3):
            row_at = lax.rem(own_at + shift + extent - 1, extent)
            weights = jnp.zeros((8, 128), F32)
            for q in range(extent):
                weights = jnp.where(source == q, kernel_rows[row_at, q], weights)
            found.append(weights)
        return found

    weights_x = top_weights(top_x, gx, lane_a, nx)
    weights_y = top_weights(top_y, gy, lane_b, ny)

    l16 = iota((16, 128), 1)
    r16 = iota((16, 128), 0)
    within = l16 - 30 * (r16 >> 2)
    keep_top = (within >= 0) & (within < 10) & (r16 < 12) & ((r16 & 3) < 3)
    from_lane = iota((128, 128), 0)
    from_lane = from_lane - 30 * ((((from_lane * 205) >> 11) * 11) >> 5)
    slot_z = jnp.where((from_lane < 10) & (iota((128, 128), 1) == 16 * gz + from_lane), 1.0, 0.0).astype(BF16)

    def contracted(received, weights, step):
        slots = received[...].reshape(8, 128)
        sums = [jnp.sum(slots * w, axis=0, keepdims=True) for w in weights]
        rows = jnp.where(slot_at == 0, sums[0], jnp.where(slot_at == 1, sums[1], sums[2]))
        return rows + pltpu.roll(rows, 128 - step, 1) + pltpu.roll(rows, 128 - 2 * step, 1)

    for n, copy in enumerate(copies_t1):
        copy.wait_recv()
    folded = contracted(rx1, weights_x, 30)
    spread_x = jnp.where(slot_at == 0, folded, jnp.where(slot_at == 1, pltpu.roll(folded, 30, 1), pltpu.roll(folded, 60, 1)))
    rx2[0] = jnp.sum(jnp.where(lane_a == slot_at, spread_x, 0.0), axis=0, keepdims=True)
    copies_t2 = top_copies(1, rx2.at[0], rx2)
    for copy in copies_t2:
        copy.start()

    for copy in copies_a:
        copy.wait_recv()

    for i in range(10):
        rx = 0.25 * (ext[2 * i + 5] + ext[2 * i + 8]) + 0.75 * (ext[2 * i + 6] + ext[2 * i + 7])
        hi, lo = split(rx)
        cells = dot(c_ry, jnp.concatenate([hi, lo], axis=0))
        fext[8 + i, 8:24, :] = cells[0:16]
        q2[i] = cells[16:24]
        if i < 8:
            q3[1, 2 * i : 2 * i + 2, :] = cells[8:10]
        if i >= 2:
            q3[0, 2 * i - 4 : 2 * i - 2, :] = cells[8:10]

    xs = {-1: pl.ds(10, 8), 0: pl.ds(8, 10), 1: pl.ds(8, 8)}
    xd = {-1: pl.ds(18, 8), 0: pl.ds(8, 10), 1: pl.ds(0, 8)}
    yd = {-1: pl.ds(24, 8), 0: pl.ds(8, 8), 1: pl.ds(0, 8)}
    copies_b = []
    for n, (dx, dy) in enumerate(NEAR):
        if dy == -1:
            src = q2.at[pl.ds(xs[dx].start - 8, xs[dx].size)]
        else:
            src = fext.at[xs[dx], pl.ds(8, 8), :]
        copies_b.append(
            remote(src, fext.at[xd[dx], yd[dy], :], b_send.at[n], b_recv.at[n], (dx, dy, 0))
        )
    for side, dx in enumerate((-1, 1)):
        copies_b.append(
            remote(q3.at[side], edge_rows.at[side, pl.ds(0, 16)], b_send.at[8 + side], b_recv.at[8 + side], (dx, 0, 0))
        )
    for copy in copies_b:
        copy.start()

    g_row = iota((32, 128), 0)
    g_cell = iota((32, 128), 1) - 1
    g_out = jnp.where(g_row < 16, g_row - 9, g_row + 47)
    g_out = jnp.where((g_row & 15) < 10, g_out, 1000)
    mains, edges = [], []
    for r in range(TERMS):
        gh, gl = split(band(1, r, zi - zo))
        ch, cl = split(dot(c_r, gh) + dot(c_r, gl))
        mains.append(dot(ch, c_rt) + dot(cl, c_rt))
        eh, el = split(band(1, r, g_cell - g_out))
        edges.append(dot(eh, c_rt) + dot(el, c_rt))
    main_h, main_l = split(jnp.concatenate(mains, axis=0))
    edge_h, edge_l = split(jnp.concatenate(edges, axis=1))

    p_at = iota((128, 64), 1)
    z_at = iota((128, 64), 0)
    cell = ((p_at - 8 * gz + 65) & 63) - 1
    spread = jnp.where(cell <= 8, composite4(z_at, cell), 0.0)
    q_at = iota((64, 128), 0)
    k_at = iota((64, 128), 1)
    picked = jnp.where((q_at == ((8 * (k_at >> 4) + (k_at & 15) + 63) & 63)) & ((k_at & 15) < 10), 1.0, 0.0)
    top_mix = dot3(dot3(spread, top_z[...]), picked)

    for copy in copies_far:
        copy.wait_recv()

    def smooth_y(source, band_y, target, at_x):
        hi, lo = split(source[at_x])
        target[at_x] = dot(band_y, jnp.concatenate([hi, hi, lo], axis=0))

    def level0_y(step, carry):
        for u in range(8):
            smooth_y(ext, band_y0, v0, step * 8 + u)
        return carry

    lax.fori_loop(0, 4, level0_y, 0)

    def smooth_x(source, target, level, count, stride):
        for r in range(TERMS):
            w = [taps[(level * TERMS + r) * 9 + k] for k in range(9)]
            for half in range(2):
                rows = slice(r * 16 + half * 8, r * 16 + half * 8 + 8)
                for x in range(count):
                    acc = w[0] * source[x + 8, rows, :]
                    for k in range(1, 9):
                        acc = acc + w[k] * (source[x + 8 - k, rows, :] + source[x + 8 + k, rows, :])
                    target[x * 16 + half * 8 : x * 16 + half * 8 + 8, r * 128 : r * 128 + 128] = acc

    smooth_x(v0, y0, 0, 16, 16)

    y0h, y0l = split(y0[...])
    eh, el = split(edge_z0)
    nt = ((1,), (1,))
    zs0[...] = dot(eh, y0h, nt) + dot(eh, y0l, nt) + dot(el, y0h, nt)
    left, right = (0, 0, -1), (0, 0, 1)
    copies_z0 = [
        remote(zs0.at[pl.ds(0, 8)], zr0.at[pl.ds(0, 8)], z_send.at[0], z_recv.at[0], left),
        remote(zs0.at[pl.ds(8, 8)], zr0.at[pl.ds(8, 8)], z_send.at[1], z_recv.at[1], right),
    ]
    for copy in copies_z0:
        copy.start()
    bh, bl = split(band_z0)
    out[...] = (dot(y0h, bh) + dot(y0h, bl) + dot(y0l, bh)).reshape(16, 16, 128)

    for copy in copies_t2:
        copy.wait_recv()
    folded = contracted(rx2, weights_y, 10)
    r16 = iota((16, 128), 0)
    wide = jnp.where((r16 & 3) == 0, folded[0:1], jnp.where((r16 & 3) == 1, folded[1:2], folded[2:3]))
    wide = jnp.where(keep_top, wide, 0.0)
    wide_h, wide_l = split(wide)
    rx3[0] = dot(wide_h, slot_z) + dot(wide_l, slot_z)
    copies_t3 = top_copies(2, rx3.at[0], rx3)
    for copy in copies_t3:
        copy.start()

    for group in (0, 1, -1):
        for copy, (dx, dy) in zip(copies_b, NEAR + [(-1, 0), (1, 0)]):
            if dx == group:
                copy.wait_recv()
        first = xd[group].start
        if group != 0:
            for x in range(8):
                rows = edge_rows[0 if group == -1 else 1, 2 * x : 2 * x + 8, :]
                fext[first + x, 16:24, :] = jnp.where(slot_at < 2, rows, 0.0)
        half = xd[group].size // 2

        def level1_y(step, carry, first=first, half=half):
            for u in range(half):
                smooth_y(fext, band_y1, v1, first + step * half + u)
            return carry

        lax.fori_loop(0, 2, level1_y, 0)

    smooth_x(v1, y1, 1, 10, 16)
    y1h, y1l = split(y1[...])
    zs1[:, 0:160] = dot(edge_h, y1h, nt) + dot(edge_h, y1l, nt) + dot(edge_l, y1h, nt)
    copies_z1 = [
        remote(zs1.at[pl.ds(0, 16)], zr1.at[pl.ds(0, 16)], z_send.at[2], z_recv.at[2], left),
        remote(zs1.at[pl.ds(16, 16)], zr1.at[pl.ds(16, 16)], z_send.at[3], z_recv.at[3], right),
    ]
    for copy in copies_z1:
        copy.start()
    level1 = dot(y1h, main_h) + dot(y1h, main_l) + dot(y1l, main_h)

    lh, ll = split(level1)
    from_cells = table[0:256, 0:160]
    potential = out[...].reshape(256, 128) + dot(from_cells, lh) + dot(from_cells, ll)

    for copy in copies_z0:
        copy.wait_recv()
    tn = ((0,), (0,))
    zh, zl = split(zr0[...])
    out[...] = (potential + dot(zh, c_sel, tn) + dot(zl, c_sel, tn)).reshape(16, 16, 128)

    for copy in copies_t3:
        copy.wait_recv()
    total = rx3[0]
    for o in range(1, nz):
        total = total + rx3[o]
    top_h, top_l = split(dot3(total, top_mix, nt))

    for copy in copies_z1:
        copy.wait_recv()
    zh, zl = split(zr1[...])
    side_h, side_l = split((dot(zh, c_edge, tn) + dot(zl, c_edge, tn))[0:160])
    late = dot(table[0:256, 0:208], jnp.concatenate([side_h, top_h, top_h, top_l], axis=0)) + dot(from_cells, side_l)
    out[...] = out[...] + late.reshape(16, 16, 128)

    for copy in copies_t1 + copies_a + copies_far + copies_t2 + copies_b + copies_t3 + copies_z0 + copies_z1:
        copy.wait_send()


def solution(mesh):
    sizes = tuple(mesh.shape[axis] for axis in AXES)
    packed = tables()

    def local(charges, exponents, amplitudes, top_x, top_y, top_z):
        vmem = pl.BlockSpec(memory_space=pltpu.VMEM)
        hbm = pl.BlockSpec(memory_space=pltpu.HBM)
        return pl.pallas_call(
            functools.partial(kernel, sizes),
            out_shape=jax.ShapeDtypeStruct(charges.shape, F32),
            in_specs=[hbm] * 7,
            out_specs=vmem,
            scratch_shapes=[
                pltpu.SMEM((2, TERMS), F32),
                pltpu.SMEM((2, TERMS), F32),
                pltpu.SMEM(top_x.shape, F32),
                pltpu.SMEM(top_y.shape, F32),
                pltpu.VMEM(top_z.shape, F32),
                pltpu.VMEM(packed.shape, BF16),
                pltpu.SemaphoreType.DMA((7,)),
                pltpu.VMEM((32, 32, 128), F32),
                pltpu.VMEM((32, 64, 128), F32),
                pltpu.VMEM((256, 512), F32),
                pltpu.VMEM((26, 32, 128), F32),
                pltpu.VMEM((10, 8, 128), F32),
                pltpu.VMEM((2, 16, 128), F32),
                pltpu.VMEM((2, 24, 128), F32),
                pltpu.VMEM((26, 64, 128), F32),
                pltpu.VMEM((160, 512), F32),
                pltpu.VMEM((8, 1, 128), F32),
                pltpu.VMEM((8, 1, 128), F32),
                pltpu.VMEM((8, 16, 128), F32),
                pltpu.VMEM((16, 256), F32),
                pltpu.VMEM((32, 256), F32),
                pltpu.VMEM((16, 256), F32),
                pltpu.VMEM((32, 256), F32),
                pltpu.VMEM((72, 8, 128), F32),
                pltpu.VMEM((8, 8, 128), F32),
                pltpu.SemaphoreType.DMA((16,)),
                pltpu.SemaphoreType.DMA((16,)),
                pltpu.SemaphoreType.DMA((10,)),
                pltpu.SemaphoreType.DMA((10,)),
                pltpu.SemaphoreType.DMA((24,)),
                pltpu.SemaphoreType.DMA((24,)),
                pltpu.SemaphoreType.DMA((4,)),
                pltpu.SemaphoreType.DMA((4,)),
            ],
            compiler_params=pltpu.CompilerParams(
                collective_id=0, has_side_effects=True, vmem_limit_bytes=40 * 2**20
            ),
        )(*[
            pltpu.with_memory_space_constraint(v, pltpu.HBM)
            for v in (charges, exponents, amplitudes, top_x, top_y, top_z, jnp.asarray(packed))
        ])

    in_specs = (P("gx", "gy", "gz"), P(), P(), P(), P(), P())
    return jax.shard_map(local, mesh=mesh, in_specs=in_specs, out_specs=P("gx", "gy", "gz"), check_vma=False)
```

```python
import functools

import jax
import jax.numpy as jnp
import numpy as np
from jax import lax
from jax.experimental import pallas as pl
from jax.experimental.pallas import tpu as pltpu
from jax.sharding import PartitionSpec as P

MESH = pl.DeviceIdType.MESH
TERMS = 4
REACH = 8
F32 = jnp.float32
BF16 = jnp.bfloat16
NEAR = [(dx, dy) for dx in (-1, 1) for dy in (-1, 1)] + [(-1, 0), (1, 0), (0, -1), (0, 1)]
AXES = ("gx", "gy", "gz")


def spline_np(off):
    off = np.asarray(off)
    return np.where((off == 1) | (off == 2), 0.75, np.where((off == 0) | (off == 3), 0.25, 0.0))


def composite_np(levels):
    box = np.ones(2**levels)
    return np.convolve(np.convolve(box, box), box) / 4.0**levels


def composite_at(levels, fine, cell):
    taps = composite_np(levels)
    off = fine - (cell * 2**levels - (2**levels - 1))
    return np.where((off >= 0) & (off < len(taps)), taps[np.clip(off, 0, len(taps) - 1)], 0.0)


def tables():
    x = np.arange(16)[:, None]
    i = np.arange(10)[None, :]
    px = spline_np(x - 2 * i + 3)
    j = np.arange(16)[None, :]
    py = np.where(j < 10, spline_np(x - 2 * j + 3), 0.0)
    pp = np.einsum("xi,yj->xyij", px, py).reshape(256, 160)
    row = np.arange(128)[:, None]
    lane = np.arange(128)[None, :]
    rt = spline_np(lane - 2 * row + 3)
    m = np.arange(24)[:, None]
    yi = np.arange(32)[None, :]
    ry = np.where(m < 10, spline_np(yi - 2 * m - 5), np.where(m >= 16, spline_np(yi - 2 * m + 23), 0.0))
    ry2 = np.concatenate([ry, ry], axis=1)
    r = np.arange(16)
    a, b = r >> 2, r & 3
    wa = composite_at(4, np.arange(16)[None, :], a[:, None] - 1) * (a < 3)[:, None]
    wb = composite_at(4, np.arange(16)[None, :], b[:, None] - 1) * (b < 3)[:, None]
    w9 = np.einsum("rx,ry->rxy", wa, wb).reshape(16, 256)
    p4 = w9.T
    mm = np.arange(32)[:, None]
    zf = np.arange(128)[None, :]
    cell = np.where(mm < 16, 55 + mm, mm - 17)
    edge = np.where((mm % 16) < 10, spline_np(zf - 2 * cell + 1), 0.0)
    t = np.arange(16)[:, None]
    sel = (zf == np.where(t < 8, 120 + t, t - 8)).astype(np.float64)
    bf = lambda v: np.asarray(v, np.float32).astype(jnp.bfloat16)
    lo = lambda v: np.asarray(v, np.float32) - bf(v).astype(np.float32)
    lanes = np.arange(128)
    lane_a, lane_b, lane_c = lanes // 30, lanes // 10 % 3, lanes % 10
    place = composite_at(4, np.arange(128)[:, None], lane_c[None, :] - 1) * (lanes < 90)
    own_row = (np.arange(16)[:, None] == (lane_a * 4 + lane_b)[None, :]) & (lanes < 90)
    packed = np.zeros((592, 256), jnp.bfloat16)
    packed[464:592, 0:128] = bf(place)
    packed[416:432, 128:256] = bf(own_row)
    packed[0:256, 0:160] = bf(pp)
    packed[0:256, 160:176] = bf(p4)
    packed[0:256, 176:192] = bf(lo(p4))
    packed[0:256, 192:208] = bf(p4)
    packed[256:384, 0:128] = bf(rt)
    packed[256:384, 128:256] = bf(rt.T)
    packed[384:416, 0:128] = bf(edge)
    packed[384:408, 128:192] = bf(ry2)
    packed[416:432, 0:128] = bf(sel)
    packed[432:448] = bf(w9)
    packed[448:464] = bf(lo(w9))
    return packed


def offsets(count, odd_far=False):
    ring = lambda o: min(o, count - o)
    return sorted(range(1, count), key=lambda o: (-(o % 2) if odd_far else 0, -ring(o)))


def split(v):
    hi = v.astype(BF16)
    return hi, (v - hi.astype(F32)).astype(BF16)


def dot(a, b, dims=((1,), (0,))):
    return lax.dot_general(a, b, (dims, ((), ())), preferred_element_type=F32)


def dot3(a, b, dims=((1,), (0,))):
    ah, al = split(a)
    bh, bl = split(b)
    return dot(ah, bh, dims) + dot(ah, bl, dims) + dot(al, bh, dims)


def iota(shape, dim):
    return lax.broadcasted_iota(jnp.int32, shape, dim)


def by_term(values, index):
    out = jnp.where(index == 0, values[0], values[1])
    for t in range(2, TERMS):
        out = jnp.where(index == t, values[t], out)
    return out


def composite4(fine, cell):
    off = fine - (cell * 16 - 15)

    def pairs(shift):
        m = jnp.maximum(off + shift, 0).astype(F32)
        return m * (m - 1.0) * 0.5

    return (pairs(2) - 3.0 * pairs(-14) + 3.0 * pairs(-30) - pairs(-46)) * (1.0 / 256.0)


def kernel(
    sizes,
    charges, exps_in, amps_in, top_x_in, top_y_in, top_z_in, table_in,
    out,
    exps, amps, top_x, top_y, top_z, table, load_sem,
    ext, v0, y0, fext, q2, q3, edge_rows, v1, y1,
    rx1, rx2, rx3,
    zs0, zs1, zr0, zr1,
    taps, inv,
    a_send, a_recv, b_send, b_recv, t_send, t_recv, z_send, z_recv,
):
    nx, ny, nz = sizes
    me = [lax.axis_index(axis) for axis in AXES]
    gx, gy, gz = me

    def at(dx, dy, dz):
        return (lax.rem(gx + dx + nx, nx), lax.rem(gy + dy + ny, ny), lax.rem(gz + dz + nz, nz))

    partners = [(0, 0, o) for o in offsets(nz, True)]
    partners += [(o, 0, 0) for o in offsets(nx) if 1 < o < nx - 1]
    partners += [(0, o, 0) for o in offsets(ny) if 1 < o < ny - 1]
    partners += [(dx, dy, 0) for dx, dy in NEAR]
    barrier = pltpu.get_barrier_semaphore()
    for p in partners:
        pl.semaphore_signal(barrier, inc=1, device_id=at(*p), device_id_type=MESH)

    loads = [
        pltpu.make_async_copy(source, target, load_sem.at[n])
        for n, (source, target) in enumerate(
            [
                (charges, ext.at[pl.ds(8, 16), pl.ds(8, 16), :]),
                (table_in, table),
                (exps_in, exps),
                (amps_in, amps),
                (top_x_in, top_x),
                (top_y_in, top_y),
                (top_z_in, top_z),
            ]
        )
    ]
    for load in loads:
        load.start()

    def remote(src, dst, send, recv, where):
        return pltpu.make_async_remote_copy(
            src_ref=src, dst_ref=dst, send_sem=send, recv_sem=recv, device_id=at(*where), device_id_type=MESH
        )

    def top_copies(step, src, dst):
        shift = [(1, 0, 0), (0, 1, 0), (0, 0, 1)][step]
        return [
            remote(
                src, dst.at[o], t_send.at[step * 8 + o], t_recv.at[step * 8 + o],
                (shift[0] * o, shift[1] * o, shift[2] * o),
            )
            for o in offsets(sizes[step], step == 2)
        ]

    zs1[...] = jnp.zeros_like(zs1)
    edge_rows[:, 16:24, :] = jnp.zeros((2, 8, 128), F32)
    for load in loads[:2]:
        load.wait()
    own = ext[8:24, 8:24, :]
    c_rt, c_r = table[256:384, 0:128], table[256:384, 128:256]
    c_edge, c_ry, c_sel = table[384:416, 0:128], table[384:408, 128:192], table[416:432, 0:128]

    flat_h, flat_l = split(own.reshape(256, 128))
    w9_h, w9_l = table[432:448, :], table[448:464, :]
    part = dot(w9_h, flat_h) + dot(w9_h, flat_l) + dot(w9_l, flat_h)
    part_h, part_l = split(part)
    place = table[464:592, 0:128]
    placed = (dot(part_h, place) + dot(part_l, place)) * table[416:432, 128:256].astype(F32)
    rx1[0] = jnp.sum(placed, axis=0, keepdims=True)

    pl.semaphore_wait(barrier, len(partners))
    source_x = {-1: [(0, 3), (3, 5)], 0: [(0, 16)], 1: [(13, 3), (8, 5)]}
    target_x = {-1: [24, 27], 0: [8], 1: [5, 0]}
    source_y = {-1: (0, 8), 0: (0, 16), 1: (8, 8)}
    target_y = {-1: 24, 0: 8, 1: 0}

    def halo_copies(part):
        found = []
        for n, (dx, dy) in enumerate(NEAR):
            if part < len(source_x[dx]):
                start, size = source_x[dx][part]
                start_y, size_y = source_y[dy]
                found.append(
                    remote(
                        charges.at[pl.ds(start, size), pl.ds(start_y, size_y), :],
                        ext.at[pl.ds(target_x[dx][part], size), pl.ds(target_y[dy], size_y), :],
                        a_send.at[part * 8 + n], a_recv.at[part * 8 + n], (dx, dy, 0),
                    )
                )
        return found

    copies_t1 = top_copies(0, rx1.at[0], rx1)
    for copy in copies_t1:
        copy.start()
    copies_a, copies_far = halo_copies(0), halo_copies(1)
    for copy in copies_a:
        copy.start()
    for copy in copies_far:
        copy.start()

    for load in loads[2:]:
        load.wait()

    for level in range(2):
        for r in range(TERMS):
            e = jnp.full((8, 128), exps[level, r], F32)
            weights = [jnp.exp(-e * float(k * k)) for k in range(REACH + 1)]
            total = weights[1]
            for k in range(2, REACH + 1):
                total = total + weights[k]
            inverse = 1.0 / (1.0 + 2.0 * total)
            inv[level * TERMS + r] = inverse
            for k in range(REACH + 1):
                taps[(level * TERMS + r) * 9 + k] = weights[k] * inverse * amps[level, r]

    def band(level, term, offset):
        if isinstance(term, int):
            e = exps[level, term]
            scale = inv[level * TERMS + term][0:1, 0:1]
        else:
            e = by_term([exps[level, t] for t in range(TERMS)], term)
            scale = by_term([inv[level * TERMS + t][0:1, 0:1] for t in range(TERMS)], term)
        far = offset.astype(F32)
        return jnp.where(jnp.abs(offset) <= REACH, jnp.exp(-e * (far * far)) * scale, 0.0)

    def tripled(matrix, copy_at):
        hi = matrix.astype(BF16)
        lo = (matrix - hi.astype(F32)).astype(BF16)
        return jnp.where(copy_at == 1, lo.astype(F32), hi.astype(F32)).astype(BF16)

    row = iota((64, 96), 0)
    col = iota((64, 96), 1)
    col32 = col & 31
    band_y0 = tripled(band(0, row >> 4, col32 - 8 - (row & 15)), col >> 5)
    where1 = jnp.where(col32 < 18, col32 - 9, jnp.where(col32 >= 24, col32 - 15, 1000))
    off1 = jnp.where((row & 15) < 10, where1 - ((row & 15) - 1), 1000)
    band_y1 = tripled(band(1, row >> 4, off1), col >> 5)

    zi = iota((128, 128), 0)
    zo = iota((128, 128), 1)
    band_z0 = jnp.concatenate([band(0, r, zi - zo) for r in range(TERMS)], axis=0)
    h_row = iota((16, 128), 0)
    h_lane = iota((16, 128), 1)
    h_out = jnp.where(h_row < 8, h_row - 8, h_row + 120)
    edge_z0 = jnp.concatenate([band(0, r, h_lane - h_out) for r in range(TERMS)], axis=1)
    slot_at = iota((8, 128), 0)
    lane_at = iota((8, 128), 1)
    tens = (lane_at * 205) >> 11
    lane_a = (tens * 11) >> 5
    lane_b = tens - 3 * lane_a

    def top_weights(kernel_rows, own_at, lane_cell, extent):
        source = (own_at - slot_at + lane_cell + extent - 1) & (extent - 1)
        found = []
        for shift in range(3):
            row_at = lax.rem(own_at + shift + extent - 1, extent)
            weights = jnp.zeros((8, 128), F32)
            for q in range(extent):
                weights = jnp.where(source == q, kernel_rows[row_at, q], weights)
            found.append(weights)
        return found

    weights_x = top_weights(top_x, gx, lane_a, nx)
    weights_y = top_weights(top_y, gy, lane_b, ny)

    l16 = iota((16, 128), 1)
    r16 = iota((16, 128), 0)
    within = l16 - 30 * (r16 >> 2)
    keep_top = (within >= 0) & (within < 10) & (r16 < 12) & ((r16 & 3) < 3)
    from_lane = iota((128, 128), 0)
    from_lane = from_lane - 30 * ((((from_lane * 205) >> 11) * 11) >> 5)
    slot_z = jnp.where((from_lane < 10) & (iota((128, 128), 1) == 16 * gz + from_lane), 1.0, 0.0).astype(BF16)

    def contracted(received, weights, step):
        slots = received[...].reshape(8, 128)
        sums = [jnp.sum(slots * w, axis=0, keepdims=True) for w in weights]
        rows = jnp.where(slot_at == 0, sums[0], jnp.where(slot_at == 1, sums[1], sums[2]))
        return rows + pltpu.roll(rows, 128 - step, 1) + pltpu.roll(rows, 128 - 2 * step, 1)

    for n, copy in enumerate(copies_t1):
        copy.wait_recv()
    folded = contracted(rx1, weights_x, 30)
    spread_x = jnp.where(slot_at == 0, folded, jnp.where(slot_at == 1, pltpu.roll(folded, 30, 1), pltpu.roll(folded, 60, 1)))
    rx2[0] = jnp.sum(jnp.where(lane_a == slot_at, spread_x, 0.0), axis=0, keepdims=True)
    copies_t2 = top_copies(1, rx2.at[0], rx2)
    for copy in copies_t2:
        copy.start()

    for copy in copies_a:
        copy.wait_recv()

    for i in range(10):
        rx = 0.25 * (ext[2 * i + 5] + ext[2 * i + 8]) + 0.75 * (ext[2 * i + 6] + ext[2 * i + 7])
        hi, lo = split(rx)
        cells = dot(c_ry, jnp.concatenate([hi, lo], axis=0))
        fext[8 + i, 8:24, :] = cells[0:16]
        q2[i] = cells[16:24]
        if i < 8:
            q3[1, 2 * i : 2 * i + 2, :] = cells[8:10]
        if i >= 2:
            q3[0, 2 * i - 4 : 2 * i - 2, :] = cells[8:10]

    xs = {-1: pl.ds(10, 8), 0: pl.ds(8, 10), 1: pl.ds(8, 8)}
    xd = {-1: pl.ds(18, 8), 0: pl.ds(8, 10), 1: pl.ds(0, 8)}
    yd = {-1: pl.ds(24, 8), 0: pl.ds(8, 8), 1: pl.ds(0, 8)}
    copies_b = []
    for n, (dx, dy) in enumerate(NEAR):
        if dy == -1:
            src = q2.at[pl.ds(xs[dx].start - 8, xs[dx].size)]
        else:
            src = fext.at[xs[dx], pl.ds(8, 8), :]
        copies_b.append(
            remote(src, fext.at[xd[dx], yd[dy], :], b_send.at[n], b_recv.at[n], (dx, dy, 0))
        )
    for side, dx in enumerate((-1, 1)):
        copies_b.append(
            remote(q3.at[side], edge_rows.at[side, pl.ds(0, 16)], b_send.at[8 + side], b_recv.at[8 + side], (dx, 0, 0))
        )
    for copy in copies_b:
        copy.start()

    g_row = iota((32, 128), 0)
    g_cell = iota((32, 128), 1) - 1
    g_out = jnp.where(g_row < 16, g_row - 9, g_row + 47)
    g_out = jnp.where((g_row & 15) < 10, g_out, 1000)
    mains, edges = [], []
    for r in range(TERMS):
        gh, gl = split(band(1, r, zi - zo))
        ch, cl = split(dot(c_r, gh) + dot(c_r, gl))
        mains.append(dot(ch, c_rt) + dot(cl, c_rt))
        eh, el = split(band(1, r, g_cell - g_out))
        edges.append(dot(eh, c_rt) + dot(el, c_rt))
    main_h, main_l = split(jnp.concatenate(mains, axis=0))
    edge_h, edge_l = split(jnp.concatenate(edges, axis=1))

    p_at = iota((128, 64), 1)
    z_at = iota((128, 64), 0)
    cell = ((p_at - 8 * gz + 65) & 63) - 1
    spread = jnp.where(cell <= 8, composite4(z_at, cell), 0.0)
    q_at = iota((64, 128), 0)
    k_at = iota((64, 128), 1)
    picked = jnp.where((q_at == ((8 * (k_at >> 4) + (k_at & 15) + 63) & 63)) & ((k_at & 15) < 10), 1.0, 0.0)
    top_mix = dot3(dot3(spread, top_z[...]), picked)

    for copy in copies_far:
        copy.wait_recv()

    def smooth_y(source, band_y, target, at_x):
        hi, lo = split(source[at_x])
        target[at_x] = dot(band_y, jnp.concatenate([hi, hi, lo], axis=0))

    def level0_y(step, carry):
        for u in range(8):
            smooth_y(ext, band_y0, v0, step * 8 + u)
        return carry

    lax.fori_loop(0, 4, level0_y, 0)

    def smooth_x(source, target, level, count, stride):
        for r in range(TERMS):
            w = [taps[(level * TERMS + r) * 9 + k] for k in range(9)]
            for half in range(2):
                rows = slice(r * 16 + half * 8, r * 16 + half * 8 + 8)
                for x in range(count):
                    acc = w[0] * source[x + 8, rows, :]
                    for k in range(1, 9):
                        acc = acc + w[k] * (source[x + 8 - k, rows, :] + source[x + 8 + k, rows, :])
                    target[x * 16 + half * 8 : x * 16 + half * 8 + 8, r * 128 : r * 128 + 128] = acc

    smooth_x(v0, y0, 0, 16, 16)

    y0h, y0l = split(y0[...])
    eh, el = split(edge_z0)
    nt = ((1,), (1,))
    zs0[...] = dot(eh, y0h, nt) + dot(eh, y0l, nt) + dot(el, y0h, nt)
    left, right = (0, 0, -1), (0, 0, 1)
    copies_z0 = [
        remote(zs0.at[pl.ds(0, 8)], zr0.at[pl.ds(0, 8)], z_send.at[0], z_recv.at[0], left),
        remote(zs0.at[pl.ds(8, 8)], zr0.at[pl.ds(8, 8)], z_send.at[1], z_recv.at[1], right),
    ]
    for copy in copies_z0:
        copy.start()
    bh, bl = split(band_z0)
    out[...] = (dot(y0h, bh) + dot(y0h, bl) + dot(y0l, bh)).reshape(16, 16, 128)

    for copy in copies_t2:
        copy.wait_recv()
    folded = contracted(rx2, weights_y, 10)
    r16 = iota((16, 128), 0)
    wide = jnp.where((r16 & 3) == 0, folded[0:1], jnp.where((r16 & 3) == 1, folded[1:2], folded[2:3]))
    wide = jnp.where(keep_top, wide, 0.0)
    wide_h, wide_l = split(wide)
    rx3[0] = dot(wide_h, slot_z) + dot(wide_l, slot_z)
    copies_t3 = top_copies(2, rx3.at[0], rx3)
    for copy in copies_t3:
        copy.start()

    for copy in copies_t1 + copies_a + copies_far + copies_t2:
        copy.wait_send()

    for group in (0, 1, -1):
        for copy, (dx, dy) in zip(copies_b, NEAR + [(-1, 0), (1, 0)]):
            if dx == group:
                copy.wait_recv()
        first = xd[group].start
        if group != 0:
            for x in range(8):
                rows = edge_rows[0 if group == -1 else 1, 2 * x : 2 * x + 8, :]
                fext[first + x, 16:24, :] = jnp.where(slot_at < 2, rows, 0.0)
        half = xd[group].size // 2

        def level1_y(step, carry, first=first, half=half):
            for u in range(half):
                smooth_y(fext, band_y1, v1, first + step * half + u)
            return carry

        lax.fori_loop(0, 2, level1_y, 0)

    smooth_x(v1, y1, 1, 10, 16)
    y1h, y1l = split(y1[...])
    zs1[:, 0:160] = dot(edge_h, y1h, nt) + dot(edge_h, y1l, nt) + dot(edge_l, y1h, nt)
    copies_z1 = [
        remote(zs1.at[pl.ds(0, 16)], zr1.at[pl.ds(0, 16)], z_send.at[2], z_recv.at[2], left),
        remote(zs1.at[pl.ds(16, 16)], zr1.at[pl.ds(16, 16)], z_send.at[3], z_recv.at[3], right),
    ]
    for copy in copies_z1:
        copy.start()
    level1 = dot(y1h, main_h) + dot(y1h, main_l) + dot(y1l, main_h)

    lh, ll = split(level1)
    from_cells = table[0:256, 0:160]
    potential = out[...].reshape(256, 128) + dot(from_cells, lh) + dot(from_cells, ll)

    for copy in copies_z0:
        copy.wait_recv()
    tn = ((0,), (0,))
    zh, zl = split(zr0[...])
    out[...] = (potential + dot(zh, c_sel, tn) + dot(zl, c_sel, tn)).reshape(16, 16, 128)

    for copy in copies_b + copies_z0 + copies_t3 + copies_z1:
        copy.wait_send()

    for copy in copies_t3:
        copy.wait_recv()
    total = rx3[0]
    for o in range(1, nz):
        total = total + rx3[o]
    top_h, top_l = split(dot3(total, top_mix, nt))

    for copy in copies_z1:
        copy.wait_recv()
    zh, zl = split(zr1[...])
    side_h, side_l = split((dot(zh, c_edge, tn) + dot(zl, c_edge, tn))[0:160])
    late = dot(table[0:256, 0:208], jnp.concatenate([side_h, top_h, top_h, top_l], axis=0)) + dot(from_cells, side_l)
    out[...] = out[...] + late.reshape(16, 16, 128)


def solution(mesh):
    sizes = tuple(mesh.shape[axis] for axis in AXES)
    packed = tables()

    def local(charges, exponents, amplitudes, top_x, top_y, top_z):
        vmem = pl.BlockSpec(memory_space=pltpu.VMEM)
        hbm = pl.BlockSpec(memory_space=pltpu.HBM)
        return pl.pallas_call(
            functools.partial(kernel, sizes),
            out_shape=jax.ShapeDtypeStruct(charges.shape, F32),
            in_specs=[hbm] * 7,
            out_specs=vmem,
            scratch_shapes=[
                pltpu.SMEM((2, TERMS), F32),
                pltpu.SMEM((2, TERMS), F32),
                pltpu.SMEM(top_x.shape, F32),
                pltpu.SMEM(top_y.shape, F32),
                pltpu.VMEM(top_z.shape, F32),
                pltpu.VMEM(packed.shape, BF16),
                pltpu.SemaphoreType.DMA((7,)),
                pltpu.VMEM((32, 32, 128), F32),
                pltpu.VMEM((32, 64, 128), F32),
                pltpu.VMEM((256, 512), F32),
                pltpu.VMEM((26, 32, 128), F32),
                pltpu.VMEM((10, 8, 128), F32),
                pltpu.VMEM((2, 16, 128), F32),
                pltpu.VMEM((2, 24, 128), F32),
                pltpu.VMEM((26, 64, 128), F32),
                pltpu.VMEM((160, 512), F32),
                pltpu.VMEM((8, 1, 128), F32),
                pltpu.VMEM((8, 1, 128), F32),
                pltpu.VMEM((8, 16, 128), F32),
                pltpu.VMEM((16, 256), F32),
                pltpu.VMEM((32, 256), F32),
                pltpu.VMEM((16, 256), F32),
                pltpu.VMEM((32, 256), F32),
                pltpu.VMEM((72, 8, 128), F32),
                pltpu.VMEM((8, 8, 128), F32),
                pltpu.SemaphoreType.DMA((16,)),
                pltpu.SemaphoreType.DMA((16,)),
                pltpu.SemaphoreType.DMA((10,)),
                pltpu.SemaphoreType.DMA((10,)),
                pltpu.SemaphoreType.DMA((24,)),
                pltpu.SemaphoreType.DMA((24,)),
                pltpu.SemaphoreType.DMA((4,)),
                pltpu.SemaphoreType.DMA((4,)),
            ],
            compiler_params=pltpu.CompilerParams(
                collective_id=0, has_side_effects=True, vmem_limit_bytes=40 * 2**20
            ),
        )(*[
            pltpu.with_memory_space_constraint(v, pltpu.HBM)
            for v in (charges, exponents, amplitudes, top_x, top_y, top_z, jnp.asarray(packed))
        ])

    in_specs = (P("gx", "gy", "gz"), P(), P(), P(), P(), P())
    return jax.shard_map(local, mesh=mesh, in_specs=in_specs, out_specs=P("gx", "gy", "gz"), check_vma=False)
```

```python
import functools

import jax
import jax.numpy as jnp
import numpy as np
from jax import lax
from jax.experimental import pallas as pl
from jax.experimental.pallas import tpu as pltpu
from jax.sharding import PartitionSpec as P

MESH = pl.DeviceIdType.MESH
TERMS = 4
REACH = 8
F32 = jnp.float32
BF16 = jnp.bfloat16
NEAR = [(dx, dy) for dx in (-1, 1) for dy in (-1, 1)] + [(-1, 0), (1, 0), (0, -1), (0, 1)]
AXES = ("gx", "gy", "gz")


def spline_np(off):
    off = np.asarray(off)
    return np.where((off == 1) | (off == 2), 0.75, np.where((off == 0) | (off == 3), 0.25, 0.0))


def composite_np(levels):
    box = np.ones(2**levels)
    return np.convolve(np.convolve(box, box), box) / 4.0**levels


def composite_at(levels, fine, cell):
    taps = composite_np(levels)
    off = fine - (cell * 2**levels - (2**levels - 1))
    return np.where((off >= 0) & (off < len(taps)), taps[np.clip(off, 0, len(taps) - 1)], 0.0)


def tables():
    x = np.arange(16)[:, None]
    i = np.arange(10)[None, :]
    px = spline_np(x - 2 * i + 3)
    j = np.arange(16)[None, :]
    py = np.where(j < 10, spline_np(x - 2 * j + 3), 0.0)
    pp = np.einsum("xi,yj->xyij", px, py).reshape(256, 160)
    row = np.arange(128)[:, None]
    lane = np.arange(128)[None, :]
    rt = spline_np(lane - 2 * row + 3)
    m = np.arange(24)[:, None]
    yi = np.arange(32)[None, :]
    ry = np.where(m < 10, spline_np(yi - 2 * m - 5), np.where(m >= 16, spline_np(yi - 2 * m + 23), 0.0))
    ry2 = np.concatenate([ry, ry], axis=1)
    r = np.arange(16)
    a, b = r >> 2, r & 3
    wa = composite_at(4, np.arange(16)[None, :], a[:, None] - 1) * (a < 3)[:, None]
    wb = composite_at(4, np.arange(16)[None, :], b[:, None] - 1) * (b < 3)[:, None]
    w9 = np.einsum("rx,ry->rxy", wa, wb).reshape(16, 256)
    p4 = w9.T
    mm = np.arange(32)[:, None]
    zf = np.arange(128)[None, :]
    cell = np.where(mm < 16, 55 + mm, mm - 17)
    edge = np.where((mm % 16) < 10, spline_np(zf - 2 * cell + 1), 0.0)
    t = np.arange(16)[:, None]
    sel = (zf == np.where(t < 8, 120 + t, t - 8)).astype(np.float64)
    bf = lambda v: np.asarray(v, np.float32).astype(jnp.bfloat16)
    lo = lambda v: np.asarray(v, np.float32) - bf(v).astype(np.float32)
    lanes = np.arange(128)
    lane_a, lane_b, lane_c = lanes // 30, lanes // 10 % 3, lanes % 10
    place = composite_at(4, np.arange(128)[:, None], lane_c[None, :] - 1) * (lanes < 90)
    own_row = (np.arange(16)[:, None] == (lane_a * 4 + lane_b)[None, :]) & (lanes < 90)
    packed = np.zeros((592, 256), jnp.bfloat16)
    packed[464:592, 0:128] = bf(place)
    packed[416:432, 128:256] = bf(own_row)
    packed[0:256, 0:160] = bf(pp)
    packed[0:256, 160:176] = bf(p4)
    packed[0:256, 176:192] = bf(lo(p4))
    packed[0:256, 192:208] = bf(p4)
    packed[256:384, 0:128] = bf(rt)
    packed[256:384, 128:256] = bf(rt.T)
    packed[384:416, 0:128] = bf(edge)
    packed[384:408, 128:192] = bf(ry2)
    packed[416:432, 0:128] = bf(sel)
    packed[432:448] = bf(w9)
    packed[448:464] = bf(lo(w9))
    return packed


def offsets(count, odd_far=False):
    ring = lambda o: min(o, count - o)
    return sorted(range(1, count), key=lambda o: (-(o % 2) if odd_far else 0, -ring(o)))


def split(v):
    hi = v.astype(BF16)
    return hi, (v - hi.astype(F32)).astype(BF16)


def dot(a, b, dims=((1,), (0,))):
    return lax.dot_general(a, b, (dims, ((), ())), preferred_element_type=F32)


def dot3(a, b, dims=((1,), (0,))):
    ah, al = split(a)
    bh, bl = split(b)
    return dot(ah, bh, dims) + dot(ah, bl, dims) + dot(al, bh, dims)


def iota(shape, dim):
    return lax.broadcasted_iota(jnp.int32, shape, dim)


def by_term(values, index):
    out = jnp.where(index == 0, values[0], values[1])
    for t in range(2, TERMS):
        out = jnp.where(index == t, values[t], out)
    return out


def composite4(fine, cell):
    off = fine - (cell * 16 - 15)

    def pairs(shift):
        m = jnp.maximum(off + shift, 0).astype(F32)
        return m * (m - 1.0) * 0.5

    return (pairs(2) - 3.0 * pairs(-14) + 3.0 * pairs(-30) - pairs(-46)) * (1.0 / 256.0)


def kernel(
    sizes,
    charges, exps_in, amps_in, top_x_in, top_y_in, top_z_in, table_in,
    out,
    exps, amps, top_x, top_y, top_z, table, load_sem,
    ext, v0, y0, fext, q2, q3, edge_rows, v1, y1,
    rx1, rx2, rx3,
    zs0, zs1, zr0, zr1,
    taps, inv,
    a_send, a_recv, b_send, b_recv, t_send, t_recv, z_send, z_recv,
):
    nx, ny, nz = sizes
    me = [lax.axis_index(axis) for axis in AXES]
    gx, gy, gz = me

    def at(dx, dy, dz):
        return (lax.rem(gx + dx + nx, nx), lax.rem(gy + dy + ny, ny), lax.rem(gz + dz + nz, nz))

    partners = [(0, 0, o) for o in offsets(nz, True)]
    partners += [(o, 0, 0) for o in offsets(nx) if 1 < o < nx - 1]
    partners += [(0, o, 0) for o in offsets(ny) if 1 < o < ny - 1]
    partners += [(dx, dy, 0) for dx, dy in NEAR]
    barrier = pltpu.get_barrier_semaphore()
    for p in partners:
        pl.semaphore_signal(barrier, inc=1, device_id=at(*p), device_id_type=MESH)

    loads = [
        pltpu.make_async_copy(source, target, load_sem.at[n])
        for n, (source, target) in enumerate(
            [
                (charges, ext.at[pl.ds(8, 16), pl.ds(8, 16), :]),
                (table_in, table),
                (exps_in, exps),
                (amps_in, amps),
                (top_x_in, top_x),
                (top_y_in, top_y),
                (top_z_in, top_z),
            ]
        )
    ]
    for load in loads:
        load.start()

    def remote(src, dst, send, recv, where):
        return pltpu.make_async_remote_copy(
            src_ref=src, dst_ref=dst, send_sem=send, recv_sem=recv, device_id=at(*where), device_id_type=MESH
        )

    def top_copies(step, src, dst):
        shift = [(1, 0, 0), (0, 1, 0), (0, 0, 1)][step]
        return [
            remote(
                src, dst.at[o], t_send.at[step * 8 + o], t_recv.at[step * 8 + o],
                (shift[0] * o, shift[1] * o, shift[2] * o),
            )
            for o in offsets(sizes[step], step == 2)
        ]

    zs1[...] = jnp.zeros_like(zs1)
    edge_rows[:, 16:24, :] = jnp.zeros((2, 8, 128), F32)
    for load in loads[:2]:
        load.wait()
    own = ext[8:24, 8:24, :]
    c_rt, c_r = table[256:384, 0:128], table[256:384, 128:256]
    c_edge, c_ry, c_sel = table[384:416, 0:128], table[384:408, 128:192], table[416:432, 0:128]

    flat_h, flat_l = split(own.reshape(256, 128))
    w9_h, w9_l = table[432:448, :], table[448:464, :]
    part = dot(w9_h, flat_h) + dot(w9_h, flat_l) + dot(w9_l, flat_h)
    part_h, part_l = split(part)
    place = table[464:592, 0:128]
    placed = (dot(part_h, place) + dot(part_l, place)) * table[416:432, 128:256].astype(F32)
    rx1[0] = jnp.sum(placed, axis=0, keepdims=True)

    pl.semaphore_wait(barrier, len(partners))
    source_x = {-1: [(0, 3), (3, 5)], 0: [(0, 16)], 1: [(13, 3), (8, 5)]}
    target_x = {-1: [24, 27], 0: [8], 1: [5, 0]}
    source_y = {-1: (0, 8), 0: (0, 16), 1: (8, 8)}
    target_y = {-1: 24, 0: 8, 1: 0}

    def halo_copies(part):
        found = []
        for n, (dx, dy) in enumerate(NEAR):
            if part < len(source_x[dx]):
                start, size = source_x[dx][part]
                start_y, size_y = source_y[dy]
                found.append(
                    remote(
                        charges.at[pl.ds(start, size), pl.ds(start_y, size_y), :],
                        ext.at[pl.ds(target_x[dx][part], size), pl.ds(target_y[dy], size_y), :],
                        a_send.at[part * 8 + n], a_recv.at[part * 8 + n], (dx, dy, 0),
                    )
                )
        return found

    copies_t1 = top_copies(0, rx1.at[0], rx1)
    for copy in copies_t1:
        copy.start()
    copies_a, copies_far = halo_copies(0), halo_copies(1)
    for copy in copies_a:
        copy.start()
    for copy in copies_far:
        copy.start()

    for load in loads[2:]:
        load.wait()

    for level in range(2):
        for r in range(TERMS):
            e = jnp.full((8, 128), exps[level, r], F32)
            weights = [jnp.exp(-e * float(k * k)) for k in range(REACH + 1)]
            total = weights[1]
            for k in range(2, REACH + 1):
                total = total + weights[k]
            inverse = 1.0 / (1.0 + 2.0 * total)
            inv[level * TERMS + r] = inverse
            for k in range(REACH + 1):
                taps[(level * TERMS + r) * 9 + k] = weights[k] * inverse * amps[level, r]

    def band(level, term, offset):
        if isinstance(term, int):
            e = exps[level, term]
            scale = inv[level * TERMS + term][0:1, 0:1]
        else:
            e = by_term([exps[level, t] for t in range(TERMS)], term)
            scale = by_term([inv[level * TERMS + t][0:1, 0:1] for t in range(TERMS)], term)
        far = offset.astype(F32)
        return jnp.where(jnp.abs(offset) <= REACH, jnp.exp(-e * (far * far)) * scale, 0.0)

    def tripled(matrix, copy_at):
        hi = matrix.astype(BF16)
        lo = (matrix - hi.astype(F32)).astype(BF16)
        return jnp.where(copy_at == 1, lo.astype(F32), hi.astype(F32)).astype(BF16)

    row = iota((64, 96), 0)
    col = iota((64, 96), 1)
    col32 = col & 31
    band_y0 = tripled(band(0, row >> 4, col32 - 8 - (row & 15)), col >> 5)
    where1 = jnp.where(col32 < 18, col32 - 9, jnp.where(col32 >= 24, col32 - 15, 1000))
    off1 = jnp.where((row & 15) < 10, where1 - ((row & 15) - 1), 1000)
    band_y1 = tripled(band(1, row >> 4, off1), col >> 5)

    zi = iota((128, 128), 0)
    zo = iota((128, 128), 1)
    band_z0 = jnp.concatenate([band(0, r, zi - zo) for r in range(TERMS)], axis=0)
    h_row = iota((16, 128), 0)
    h_lane = iota((16, 128), 1)
    h_out = jnp.where(h_row < 8, h_row - 8, h_row + 120)
    edge_z0 = jnp.concatenate([band(0, r, h_lane - h_out) for r in range(TERMS)], axis=1)
    slot_at = iota((8, 128), 0)
    lane_at = iota((8, 128), 1)
    tens = (lane_at * 205) >> 11
    lane_a = (tens * 11) >> 5
    lane_b = tens - 3 * lane_a

    def top_weights(kernel_rows, own_at, lane_cell, extent):
        source = (own_at - slot_at + lane_cell + extent - 1) & (extent - 1)
        found = []
        for shift in range(3):
            row_at = lax.rem(own_at + shift + extent - 1, extent)
            weights = jnp.zeros((8, 128), F32)
            for q in range(extent):
                weights = jnp.where(source == q, kernel_rows[row_at, q], weights)
            found.append(weights)
        return found

    weights_x = top_weights(top_x, gx, lane_a, nx)
    weights_y = top_weights(top_y, gy, lane_b, ny)

    l16 = iota((16, 128), 1)
    r16 = iota((16, 128), 0)
    within = l16 - 30 * (r16 >> 2)
    keep_top = (within >= 0) & (within < 10) & (r16 < 12) & ((r16 & 3) < 3)
    from_lane = iota((128, 128), 0)
    from_lane = from_lane - 30 * ((((from_lane * 205) >> 11) * 11) >> 5)
    slot_z = jnp.where((from_lane < 10) & (iota((128, 128), 1) == 16 * gz + from_lane), 1.0, 0.0).astype(BF16)

    def contracted(received, weights, step):
        slots = received[...].reshape(8, 128)
        sums = [jnp.sum(slots * w, axis=0, keepdims=True) for w in weights]
        rows = jnp.where(slot_at == 0, sums[0], jnp.where(slot_at == 1, sums[1], sums[2]))
        return rows + pltpu.roll(rows, 128 - step, 1) + pltpu.roll(rows, 128 - 2 * step, 1)

    for n, copy in enumerate(copies_t1):
        copy.wait_recv()
    folded = contracted(rx1, weights_x, 30)
    spread_x = jnp.where(slot_at == 0, folded, jnp.where(slot_at == 1, pltpu.roll(folded, 30, 1), pltpu.roll(folded, 60, 1)))
    rx2[0] = jnp.sum(jnp.where(lane_a == slot_at, spread_x, 0.0), axis=0, keepdims=True)
    copies_t2 = top_copies(1, rx2.at[0], rx2)
    for copy in copies_t2:
        copy.start()

    for copy in copies_a:
        copy.wait_recv()

    for i in range(10):
        rx = 0.25 * (ext[2 * i + 5] + ext[2 * i + 8]) + 0.75 * (ext[2 * i + 6] + ext[2 * i + 7])
        hi, lo = split(rx)
        cells = dot(c_ry, jnp.concatenate([hi, lo], axis=0))
        fext[8 + i, 8:24, :] = cells[0:16]
        q2[i] = cells[16:24]
        if i < 8:
            q3[1, 2 * i : 2 * i + 2, :] = cells[8:10]
        if i >= 2:
            q3[0, 2 * i - 4 : 2 * i - 2, :] = cells[8:10]

    xs = {-1: pl.ds(10, 8), 0: pl.ds(8, 10), 1: pl.ds(8, 8)}
    xd = {-1: pl.ds(18, 8), 0: pl.ds(8, 10), 1: pl.ds(0, 8)}
    yd = {-1: pl.ds(24, 8), 0: pl.ds(8, 8), 1: pl.ds(0, 8)}
    copies_b = []
    for n, (dx, dy) in enumerate(NEAR):
        if dy == -1:
            src = q2.at[pl.ds(xs[dx].start - 8, xs[dx].size)]
        else:
            src = fext.at[xs[dx], pl.ds(8, 8), :]
        copies_b.append(
            remote(src, fext.at[xd[dx], yd[dy], :], b_send.at[n], b_recv.at[n], (dx, dy, 0))
        )
    for side, dx in enumerate((-1, 1)):
        copies_b.append(
            remote(q3.at[side], edge_rows.at[side, pl.ds(0, 16)], b_send.at[8 + side], b_recv.at[8 + side], (dx, 0, 0))
        )
    for copy in copies_b:
        copy.start()

    g_row = iota((32, 128), 0)
    g_cell = iota((32, 128), 1) - 1
    g_out = jnp.where(g_row < 16, g_row - 9, g_row + 47)
    g_out = jnp.where((g_row & 15) < 10, g_out, 1000)
    mains, edges = [], []
    for r in range(TERMS):
        gh, gl = split(band(1, r, zi - zo))
        ch, cl = split(dot(c_r, gh) + dot(c_r, gl))
        mains.append(dot(ch, c_rt) + dot(cl, c_rt))
        eh, el = split(band(1, r, g_cell - g_out))
        edges.append(dot(eh, c_rt) + dot(el, c_rt))
    main_h, main_l = split(jnp.concatenate(mains, axis=0))
    edge_h, edge_l = split(jnp.concatenate(edges, axis=1))

    p_at = iota((128, 64), 1)
    z_at = iota((128, 64), 0)
    cell = ((p_at - 8 * gz + 65) & 63) - 1
    spread = jnp.where(cell <= 8, composite4(z_at, cell), 0.0)
    q_at = iota((64, 128), 0)
    k_at = iota((64, 128), 1)
    picked = jnp.where((q_at == ((8 * (k_at >> 4) + (k_at & 15) + 63) & 63)) & ((k_at & 15) < 10), 1.0, 0.0)
    top_mix = dot3(dot3(spread, top_z[...]), picked)

    for copy in copies_far:
        copy.wait_recv()

    def smooth_y(source, band_y, target, at_x):
        hi, lo = split(source[at_x])
        target[at_x] = dot(band_y, jnp.concatenate([hi, hi, lo], axis=0))

    def level0_y(step, carry):
        for u in range(8):
            smooth_y(ext, band_y0, v0, step * 8 + u)
        return carry

    lax.fori_loop(0, 4, level0_y, 0)

    def smooth_x(source, target, level, count, terms):
        for r in terms:
            w = [taps[(level * TERMS + r) * 9 + k] for k in range(9)]
            for half in range(2):
                rows = slice(r * 16 + half * 8, r * 16 + half * 8 + 8)
                for x in range(count):
                    acc = w[0] * source[x + 8, rows, :]
                    for k in range(1, 9):
                        acc = acc + w[k] * (source[x + 8 - k, rows, :] + source[x + 8 + k, rows, :])
                    target[x * 16 + half * 8 : x * 16 + half * 8 + 8, r * 128 : r * 128 + 128] = acc

    smooth_x(v0, y0, 0, 16, range(TERMS))

    y0h, y0l = split(y0[...])
    eh, el = split(edge_z0)
    nt = ((1,), (1,))
    zs0[...] = dot(eh, y0h, nt) + dot(eh, y0l, nt) + dot(el, y0h, nt)
    left, right = (0, 0, -1), (0, 0, 1)
    copies_z0 = [
        remote(zs0.at[pl.ds(0, 8)], zr0.at[pl.ds(0, 8)], z_send.at[0], z_recv.at[0], left),
        remote(zs0.at[pl.ds(8, 8)], zr0.at[pl.ds(8, 8)], z_send.at[1], z_recv.at[1], right),
    ]
    for copy in copies_z0:
        copy.start()
    bh, bl = split(band_z0)
    out[...] = (dot(y0h, bh) + dot(y0h, bl) + dot(y0l, bh)).reshape(16, 16, 128)

    for copy in copies_t2:
        copy.wait_recv()
    folded = contracted(rx2, weights_y, 10)
    r16 = iota((16, 128), 0)
    wide = jnp.where((r16 & 3) == 0, folded[0:1], jnp.where((r16 & 3) == 1, folded[1:2], folded[2:3]))
    wide = jnp.where(keep_top, wide, 0.0)
    wide_h, wide_l = split(wide)
    rx3[0] = dot(wide_h, slot_z) + dot(wide_l, slot_z)
    copies_t3 = top_copies(2, rx3.at[0], rx3)
    for copy in copies_t3:
        copy.start()

    for copy in copies_t1 + copies_a + copies_far + copies_t2:
        copy.wait_send()

    for group in (0, 1, -1):
        for copy, (dx, dy) in zip(copies_b, NEAR + [(-1, 0), (1, 0)]):
            if dx == group:
                copy.wait_recv()
        first = xd[group].start
        if group != 0:
            for x in range(8):
                rows = edge_rows[0 if group == -1 else 1, 2 * x : 2 * x + 8, :]
                fext[first + x, 16:24, :] = jnp.where(slot_at < 2, rows, 0.0)
        half = xd[group].size // 2

        def level1_y(step, carry, first=first, half=half):
            for u in range(half):
                smooth_y(fext, band_y1, v1, first + step * half + u)
            return carry

        lax.fori_loop(0, 2, level1_y, 0)

    pairs, beyond = [], jnp.zeros((32, 160), F32)
    for first in (0, 2):
        smooth_x(v1, y1, 1, 10, (first, first + 1))
        part = slice(first * 128, first * 128 + 256)
        hi, lo = split(y1[:, part])
        beyond = beyond + dot(edge_h[:, part], hi, nt) + dot(edge_h[:, part], lo, nt) + dot(edge_l[:, part], hi, nt)
        pairs.append((hi, lo))
    zs1[:, 0:160] = beyond
    y1h = jnp.concatenate([hi for hi, _ in pairs], axis=1)
    y1l = jnp.concatenate([lo for _, lo in pairs], axis=1)
    copies_z1 = [
        remote(zs1.at[pl.ds(0, 16)], zr1.at[pl.ds(0, 16)], z_send.at[2], z_recv.at[2], left),
        remote(zs1.at[pl.ds(16, 16)], zr1.at[pl.ds(16, 16)], z_send.at[3], z_recv.at[3], right),
    ]
    for copy in copies_z1:
        copy.start()
    level1 = dot(y1h, main_h) + dot(y1h, main_l) + dot(y1l, main_h)

    lh, ll = split(level1)
    from_cells = table[0:256, 0:160]
    potential = out[...].reshape(256, 128) + dot(from_cells, lh) + dot(from_cells, ll)

    for copy in copies_z0:
        copy.wait_recv()
    tn = ((0,), (0,))
    zh, zl = split(zr0[...])
    out[...] = (potential + dot(zh, c_sel, tn) + dot(zl, c_sel, tn)).reshape(16, 16, 128)

    for copy in copies_b + copies_z0 + copies_t3 + copies_z1:
        copy.wait_send()

    for copy in copies_t3:
        copy.wait_recv()
    total = rx3[0]
    for o in range(1, nz):
        total = total + rx3[o]
    top_h, top_l = split(dot3(total, top_mix, nt))

    for copy in copies_z1:
        copy.wait_recv()
    zh, zl = split(zr1[...])
    side_h, side_l = split((dot(zh, c_edge, tn) + dot(zl, c_edge, tn))[0:160])
    late = dot(table[0:256, 0:208], jnp.concatenate([side_h, top_h, top_h, top_l], axis=0)) + dot(from_cells, side_l)
    out[...] = out[...] + late.reshape(16, 16, 128)


def solution(mesh):
    sizes = tuple(mesh.shape[axis] for axis in AXES)
    packed = tables()

    def local(charges, exponents, amplitudes, top_x, top_y, top_z):
        vmem = pl.BlockSpec(memory_space=pltpu.VMEM)
        hbm = pl.BlockSpec(memory_space=pltpu.HBM)
        return pl.pallas_call(
            functools.partial(kernel, sizes),
            out_shape=jax.ShapeDtypeStruct(charges.shape, F32),
            in_specs=[hbm] * 7,
            out_specs=vmem,
            scratch_shapes=[
                pltpu.SMEM((2, TERMS), F32),
                pltpu.SMEM((2, TERMS), F32),
                pltpu.SMEM(top_x.shape, F32),
                pltpu.SMEM(top_y.shape, F32),
                pltpu.VMEM(top_z.shape, F32),
                pltpu.VMEM(packed.shape, BF16),
                pltpu.SemaphoreType.DMA((7,)),
                pltpu.VMEM((32, 32, 128), F32),
                pltpu.VMEM((32, 64, 128), F32),
                pltpu.VMEM((256, 512), F32),
                pltpu.VMEM((26, 32, 128), F32),
                pltpu.VMEM((10, 8, 128), F32),
                pltpu.VMEM((2, 16, 128), F32),
                pltpu.VMEM((2, 24, 128), F32),
                pltpu.VMEM((26, 64, 128), F32),
                pltpu.VMEM((160, 512), F32),
                pltpu.VMEM((8, 1, 128), F32),
                pltpu.VMEM((8, 1, 128), F32),
                pltpu.VMEM((8, 16, 128), F32),
                pltpu.VMEM((16, 256), F32),
                pltpu.VMEM((32, 256), F32),
                pltpu.VMEM((16, 256), F32),
                pltpu.VMEM((32, 256), F32),
                pltpu.VMEM((72, 8, 128), F32),
                pltpu.VMEM((8, 8, 128), F32),
                pltpu.SemaphoreType.DMA((16,)),
                pltpu.SemaphoreType.DMA((16,)),
                pltpu.SemaphoreType.DMA((10,)),
                pltpu.SemaphoreType.DMA((10,)),
                pltpu.SemaphoreType.DMA((24,)),
                pltpu.SemaphoreType.DMA((24,)),
                pltpu.SemaphoreType.DMA((4,)),
                pltpu.SemaphoreType.DMA((4,)),
            ],
            compiler_params=pltpu.CompilerParams(
                collective_id=0, has_side_effects=True, vmem_limit_bytes=40 * 2**20
            ),
        )(*[
            pltpu.with_memory_space_constraint(v, pltpu.HBM)
            for v in (charges, exponents, amplitudes, top_x, top_y, top_z, jnp.asarray(packed))
        ])

    in_specs = (P("gx", "gy", "gz"), P(), P(), P(), P(), P())
    return jax.shard_map(local, mesh=mesh, in_specs=in_specs, out_specs=P("gx", "gy", "gz"), check_vma=False)
```

```python
import functools

import jax
import jax.numpy as jnp
import numpy as np
from jax import lax
from jax.experimental import pallas as pl
from jax.experimental.pallas import tpu as pltpu
from jax.sharding import PartitionSpec as P

MESH = pl.DeviceIdType.MESH
TERMS = 4
REACH = 8
F32 = jnp.float32
BF16 = jnp.bfloat16
NEAR = [(dx, dy) for dx in (-1, 1) for dy in (-1, 1)] + [(-1, 0), (1, 0), (0, -1), (0, 1)]
AXES = ("gx", "gy", "gz")


def spline_np(off):
    off = np.asarray(off)
    return np.where((off == 1) | (off == 2), 0.75, np.where((off == 0) | (off == 3), 0.25, 0.0))


def composite_np(levels):
    box = np.ones(2**levels)
    return np.convolve(np.convolve(box, box), box) / 4.0**levels


def composite_at(levels, fine, cell):
    taps = composite_np(levels)
    off = fine - (cell * 2**levels - (2**levels - 1))
    return np.where((off >= 0) & (off < len(taps)), taps[np.clip(off, 0, len(taps) - 1)], 0.0)


def tables():
    x = np.arange(16)[:, None]
    i = np.arange(10)[None, :]
    px = spline_np(x - 2 * i + 3)
    j = np.arange(16)[None, :]
    py = np.where(j < 10, spline_np(x - 2 * j + 3), 0.0)
    pp = np.einsum("xi,yj->xyij", px, py).reshape(256, 160)
    row = np.arange(128)[:, None]
    lane = np.arange(128)[None, :]
    rt = spline_np(lane - 2 * row + 3)
    m = np.arange(24)[:, None]
    yi = np.arange(32)[None, :]
    ry = np.where(m < 10, spline_np(yi - 2 * m - 5), np.where(m >= 16, spline_np(yi - 2 * m + 23), 0.0))
    ry2 = np.concatenate([ry, ry], axis=1)
    r = np.arange(16)
    a, b = r >> 2, r & 3
    wa = composite_at(4, np.arange(16)[None, :], a[:, None] - 1) * (a < 3)[:, None]
    wb = composite_at(4, np.arange(16)[None, :], b[:, None] - 1) * (b < 3)[:, None]
    w9 = np.einsum("rx,ry->rxy", wa, wb).reshape(16, 256)
    p4 = w9.T
    mm = np.arange(32)[:, None]
    zf = np.arange(128)[None, :]
    cell = np.where(mm < 16, 55 + mm, mm - 17)
    edge = np.where((mm % 16) < 10, spline_np(zf - 2 * cell + 1), 0.0)
    t = np.arange(16)[:, None]
    sel = (zf == np.where(t < 8, 120 + t, t - 8)).astype(np.float64)
    bf = lambda v: np.asarray(v, np.float32).astype(jnp.bfloat16)
    lo = lambda v: np.asarray(v, np.float32) - bf(v).astype(np.float32)
    lanes = np.arange(128)
    lane_a, lane_b, lane_c = lanes // 30, lanes // 10 % 3, lanes % 10
    place = composite_at(4, np.arange(128)[:, None], lane_c[None, :] - 1) * (lanes < 90)
    own_row = (np.arange(16)[:, None] == (lane_a * 4 + lane_b)[None, :]) & (lanes < 90)
    packed = np.zeros((592, 256), jnp.bfloat16)
    packed[464:592, 0:128] = bf(place)
    packed[416:432, 128:256] = bf(own_row)
    packed[0:256, 0:160] = bf(pp)
    packed[0:256, 160:176] = bf(p4)
    packed[0:256, 176:192] = bf(lo(p4))
    packed[0:256, 192:208] = bf(p4)
    packed[256:384, 0:128] = bf(rt)
    packed[256:384, 128:256] = bf(rt.T)
    packed[384:416, 0:128] = bf(edge)
    packed[384:408, 128:192] = bf(ry2)
    packed[416:432, 0:128] = bf(sel)
    packed[432:448] = bf(w9)
    packed[448:464] = bf(lo(w9))
    return packed


def offsets(count, odd_far=False):
    ring = lambda o: min(o, count - o)
    return sorted(range(1, count), key=lambda o: (-(o % 2) if odd_far else 0, -ring(o)))


def split(v):
    hi = v.astype(BF16)
    return hi, (v - hi.astype(F32)).astype(BF16)


def dot(a, b, dims=((1,), (0,))):
    return lax.dot_general(a, b, (dims, ((), ())), preferred_element_type=F32)


def dot3(a, b, dims=((1,), (0,))):
    ah, al = split(a)
    bh, bl = split(b)
    return dot(ah, bh, dims) + dot(ah, bl, dims) + dot(al, bh, dims)


def iota(shape, dim):
    return lax.broadcasted_iota(jnp.int32, shape, dim)


def by_term(values, index):
    out = jnp.where(index == 0, values[0], values[1])
    for t in range(2, TERMS):
        out = jnp.where(index == t, values[t], out)
    return out


def composite4(fine, cell):
    off = fine - (cell * 16 - 15)

    def pairs(shift):
        m = jnp.maximum(off + shift, 0).astype(F32)
        return m * (m - 1.0) * 0.5

    return (pairs(2) - 3.0 * pairs(-14) + 3.0 * pairs(-30) - pairs(-46)) * (1.0 / 256.0)


def kernel(
    sizes,
    charges, exps_in, amps_in, top_x_in, top_y_in, top_z_in, table_in,
    out,
    exps, amps, top_x, top_y, top_z, table, load_sem,
    ext, v0, y0, fext, q2, q3, edge_rows, v1, y1,
    rx1, rx2, rx3,
    zs0, zs1, zr0, zr1,
    taps, inv,
    a_send, a_recv, b_send, b_recv, t_send, t_recv, z_send, z_recv,
):
    nx, ny, nz = sizes
    me = [lax.axis_index(axis) for axis in AXES]
    gx, gy, gz = me

    def at(dx, dy, dz):
        return (lax.rem(gx + dx + nx, nx), lax.rem(gy + dy + ny, ny), lax.rem(gz + dz + nz, nz))

    loads = [
        pltpu.make_async_copy(source, target, load_sem.at[n])
        for n, (source, target) in enumerate(
            [
                (charges, ext.at[pl.ds(8, 16), pl.ds(8, 16), :]),
                (table_in, table),
                (exps_in, exps),
                (amps_in, amps),
                (top_x_in, top_x),
                (top_y_in, top_y),
                (top_z_in, top_z),
            ]
        )
    ]
    for load in loads[:2]:
        load.start()

    partners = [(0, 0, o) for o in offsets(nz, True)]
    partners += [(o, 0, 0) for o in offsets(nx) if 1 < o < nx - 1]
    partners += [(0, o, 0) for o in offsets(ny) if 1 < o < ny - 1]
    partners += [(dx, dy, 0) for dx, dy in NEAR]
    barrier = pltpu.get_barrier_semaphore()
    for p in partners:
        pl.semaphore_signal(barrier, inc=1, device_id=at(*p), device_id_type=MESH)

    for load in loads[2:]:
        load.start()

    def remote(src, dst, send, recv, where):
        return pltpu.make_async_remote_copy(
            src_ref=src, dst_ref=dst, send_sem=send, recv_sem=recv, device_id=at(*where), device_id_type=MESH
        )

    def top_copies(step, src, dst):
        shift = [(1, 0, 0), (0, 1, 0), (0, 0, 1)][step]
        return [
            remote(
                src, dst.at[o], t_send.at[step * 8 + o], t_recv.at[step * 8 + o],
                (shift[0] * o, shift[1] * o, shift[2] * o),
            )
            for o in offsets(sizes[step], step == 2)
        ]

    zs1[...] = jnp.zeros_like(zs1)
    edge_rows[:, 16:24, :] = jnp.zeros((2, 8, 128), F32)
    for load in loads[:2]:
        load.wait()
    own = ext[8:24, 8:24, :]
    c_rt, c_r = table[256:384, 0:128], table[256:384, 128:256]
    c_edge, c_ry, c_sel = table[384:416, 0:128], table[384:408, 128:192], table[416:432, 0:128]

    flat_h, flat_l = split(own.reshape(256, 128))
    w9_h, w9_l = table[432:448, :], table[448:464, :]
    part = dot(w9_h, flat_h) + dot(w9_h, flat_l) + dot(w9_l, flat_h)
    part_h, part_l = split(part)
    place = table[464:592, 0:128]
    placed = (dot(part_h, place) + dot(part_l, place)) * table[416:432, 128:256].astype(F32)
    rx1[0] = jnp.sum(placed, axis=0, keepdims=True)

    pl.semaphore_wait(barrier, len(partners))
    source_x = {-1: [(0, 3), (3, 5)], 0: [(0, 16)], 1: [(13, 3), (8, 5)]}
    target_x = {-1: [24, 27], 0: [8], 1: [5, 0]}
    source_y = {-1: (0, 8), 0: (0, 16), 1: (8, 8)}
    target_y = {-1: 24, 0: 8, 1: 0}

    def halo_copies(part):
        found = []
        for n, (dx, dy) in enumerate(NEAR):
            if part < len(source_x[dx]):
                start, size = source_x[dx][part]
                start_y, size_y = source_y[dy]
                found.append(
                    remote(
                        charges.at[pl.ds(start, size), pl.ds(start_y, size_y), :],
                        ext.at[pl.ds(target_x[dx][part], size), pl.ds(target_y[dy], size_y), :],
                        a_send.at[part * 8 + n], a_recv.at[part * 8 + n], (dx, dy, 0),
                    )
                )
        return found

    copies_t1 = top_copies(0, rx1.at[0], rx1)
    for copy in copies_t1:
        copy.start()
    copies_a, copies_far = halo_copies(0), halo_copies(1)
    for copy in copies_a:
        copy.start()
    for copy in copies_far:
        copy.start()

    for load in loads[2:]:
        load.wait()

    for level in range(2):
        for r in range(TERMS):
            e = jnp.full((8, 128), exps[level, r], F32)
            weights = [jnp.exp(-e * float(k * k)) for k in range(REACH + 1)]
            total = weights[1]
            for k in range(2, REACH + 1):
                total = total + weights[k]
            inverse = 1.0 / (1.0 + 2.0 * total)
            inv[level * TERMS + r] = inverse
            for k in range(REACH + 1):
                taps[(level * TERMS + r) * 9 + k] = weights[k] * inverse * amps[level, r]

    def band(level, term, offset):
        if isinstance(term, int):
            e = exps[level, term]
            scale = inv[level * TERMS + term][0:1, 0:1]
        else:
            e = by_term([exps[level, t] for t in range(TERMS)], term)
            scale = by_term([inv[level * TERMS + t][0:1, 0:1] for t in range(TERMS)], term)
        far = offset.astype(F32)
        return jnp.where(jnp.abs(offset) <= REACH, jnp.exp(-e * (far * far)) * scale, 0.0)

    def tripled(matrix, copy_at):
        hi = matrix.astype(BF16)
        lo = (matrix - hi.astype(F32)).astype(BF16)
        return jnp.where(copy_at == 1, lo.astype(F32), hi.astype(F32)).astype(BF16)

    row = iota((64, 96), 0)
    col = iota((64, 96), 1)
    col32 = col & 31
    band_y0 = tripled(band(0, row >> 4, col32 - 8 - (row & 15)), col >> 5)
    where1 = jnp.where(col32 < 18, col32 - 9, jnp.where(col32 >= 24, col32 - 15, 1000))
    off1 = jnp.where((row & 15) < 10, where1 - ((row & 15) - 1), 1000)
    band_y1 = tripled(band(1, row >> 4, off1), col >> 5)

    zi = iota((128, 128), 0)
    zo = iota((128, 128), 1)
    band_z0 = jnp.concatenate([band(0, r, zi - zo) for r in range(TERMS)], axis=0)
    h_row = iota((16, 128), 0)
    h_lane = iota((16, 128), 1)
    h_out = jnp.where(h_row < 8, h_row - 8, h_row + 120)
    edge_z0 = jnp.concatenate([band(0, r, h_lane - h_out) for r in range(TERMS)], axis=1)
    slot_at = iota((8, 128), 0)
    lane_at = iota((8, 128), 1)
    tens = (lane_at * 205) >> 11
    lane_a = (tens * 11) >> 5
    lane_b = tens - 3 * lane_a

    def top_weights(kernel_rows, own_at, lane_cell, extent):
        source = (own_at - slot_at + lane_cell + extent - 1) & (extent - 1)
        found = []
        for shift in range(3):
            row_at = lax.rem(own_at + shift + extent - 1, extent)
            weights = jnp.zeros((8, 128), F32)
            for q in range(extent):
                weights = jnp.where(source == q, kernel_rows[row_at, q], weights)
            found.append(weights)
        return found

    weights_x = top_weights(top_x, gx, lane_a, nx)
    weights_y = top_weights(top_y, gy, lane_b, ny)

    l16 = iota((16, 128), 1)
    r16 = iota((16, 128), 0)
    within = l16 - 30 * (r16 >> 2)
    keep_top = (within >= 0) & (within < 10) & (r16 < 12) & ((r16 & 3) < 3)
    from_lane = iota((128, 128), 0)
    from_lane = from_lane - 30 * ((((from_lane * 205) >> 11) * 11) >> 5)
    slot_z = jnp.where((from_lane < 10) & (iota((128, 128), 1) == 16 * gz + from_lane), 1.0, 0.0).astype(BF16)

    def contracted(received, weights, step):
        slots = received[...].reshape(8, 128)
        sums = [jnp.sum(slots * w, axis=0, keepdims=True) for w in weights]
        rows = jnp.where(slot_at == 0, sums[0], jnp.where(slot_at == 1, sums[1], sums[2]))
        return rows + pltpu.roll(rows, 128 - step, 1) + pltpu.roll(rows, 128 - 2 * step, 1)

    for n, copy in enumerate(copies_t1):
        copy.wait_recv()
    folded = contracted(rx1, weights_x, 30)
    spread_x = jnp.where(slot_at == 0, folded, jnp.where(slot_at == 1, pltpu.roll(folded, 30, 1), pltpu.roll(folded, 60, 1)))
    rx2[0] = jnp.sum(jnp.where(lane_a == slot_at, spread_x, 0.0), axis=0, keepdims=True)
    copies_t2 = top_copies(1, rx2.at[0], rx2)
    for copy in copies_t2:
        copy.start()

    for copy in copies_a:
        copy.wait_recv()

    for i in range(10):
        rx = 0.25 * (ext[2 * i + 5] + ext[2 * i + 8]) + 0.75 * (ext[2 * i + 6] + ext[2 * i + 7])
        hi, lo = split(rx)
        cells = dot(c_ry, jnp.concatenate([hi, lo], axis=0))
        fext[8 + i, 8:24, :] = cells[0:16]
        q2[i] = cells[16:24]
        if i < 8:
            q3[1, 2 * i : 2 * i + 2, :] = cells[8:10]
        if i >= 2:
            q3[0, 2 * i - 4 : 2 * i - 2, :] = cells[8:10]

    xs = {-1: pl.ds(10, 8), 0: pl.ds(8, 10), 1: pl.ds(8, 8)}
    xd = {-1: pl.ds(18, 8), 0: pl.ds(8, 10), 1: pl.ds(0, 8)}
    yd = {-1: pl.ds(24, 8), 0: pl.ds(8, 8), 1: pl.ds(0, 8)}
    copies_b = []
    for n, (dx, dy) in enumerate(NEAR):
        if dy == -1:
            src = q2.at[pl.ds(xs[dx].start - 8, xs[dx].size)]
        else:
            src = fext.at[xs[dx], pl.ds(8, 8), :]
        copies_b.append(
            remote(src, fext.at[xd[dx], yd[dy], :], b_send.at[n], b_recv.at[n], (dx, dy, 0))
        )
    for side, dx in enumerate((-1, 1)):
        copies_b.append(
            remote(q3.at[side], edge_rows.at[side, pl.ds(0, 16)], b_send.at[8 + side], b_recv.at[8 + side], (dx, 0, 0))
        )
    for copy in copies_b:
        copy.start()

    g_row = iota((32, 128), 0)
    g_cell = iota((32, 128), 1) - 1
    g_out = jnp.where(g_row < 16, g_row - 9, g_row + 47)
    g_out = jnp.where((g_row & 15) < 10, g_out, 1000)
    mains, edges = [], []
    for r in range(TERMS):
        gh, gl = split(band(1, r, zi - zo))
        ch, cl = split(dot(c_r, gh) + dot(c_r, gl))
        mains.append(dot(ch, c_rt) + dot(cl, c_rt))
        eh, el = split(band(1, r, g_cell - g_out))
        edges.append(dot(eh, c_rt) + dot(el, c_rt))
    main_h, main_l = split(jnp.concatenate(mains, axis=0))
    edge_h, edge_l = split(jnp.concatenate(edges, axis=1))

    p_at = iota((128, 64), 1)
    z_at = iota((128, 64), 0)
    cell = ((p_at - 8 * gz + 65) & 63) - 1
    spread = jnp.where(cell <= 8, composite4(z_at, cell), 0.0)
    q_at = iota((64, 128), 0)
    k_at = iota((64, 128), 1)
    picked = jnp.where((q_at == ((8 * (k_at >> 4) + (k_at & 15) + 63) & 63)) & ((k_at & 15) < 10), 1.0, 0.0)
    top_mix = dot3(dot3(spread, top_z[...]), picked)

    for copy in copies_far:
        copy.wait_recv()

    def smooth_y(source, band_y, target, at_x):
        hi, lo = split(source[at_x])
        target[at_x] = dot(band_y, jnp.concatenate([hi, hi, lo], axis=0))

    def level0_y(step, carry):
        for u in range(8):
            smooth_y(ext, band_y0, v0, step * 8 + u)
        return carry

    lax.fori_loop(0, 4, level0_y, 0)

    def smooth_x(source, target, level, count, terms):
        for r in terms:
            w = [taps[(level * TERMS + r) * 9 + k] for k in range(9)]
            for half in range(2):
                rows = slice(r * 16 + half * 8, r * 16 + half * 8 + 8)
                for x in range(count):
                    acc = w[0] * source[x + 8, rows, :]
                    for k in range(1, 9):
                        acc = acc + w[k] * (source[x + 8 - k, rows, :] + source[x + 8 + k, rows, :])
                    target[x * 16 + half * 8 : x * 16 + half * 8 + 8, r * 128 : r * 128 + 128] = acc

    smooth_x(v0, y0, 0, 16, range(TERMS))

    y0h, y0l = split(y0[...])
    eh, el = split(edge_z0)
    nt = ((1,), (1,))
    zs0[...] = dot(eh, y0h, nt) + dot(eh, y0l, nt) + dot(el, y0h, nt)
    left, right = (0, 0, -1), (0, 0, 1)
    copies_z0 = [
        remote(zs0.at[pl.ds(0, 8)], zr0.at[pl.ds(0, 8)], z_send.at[0], z_recv.at[0], left),
        remote(zs0.at[pl.ds(8, 8)], zr0.at[pl.ds(8, 8)], z_send.at[1], z_recv.at[1], right),
    ]
    for copy in copies_z0:
        copy.start()
    bh, bl = split(band_z0)
    out[...] = (dot(y0h, bh) + dot(y0h, bl) + dot(y0l, bh)).reshape(16, 16, 128)

    for copy in copies_t2:
        copy.wait_recv()
    folded = contracted(rx2, weights_y, 10)
    r16 = iota((16, 128), 0)
    wide = jnp.where((r16 & 3) == 0, folded[0:1], jnp.where((r16 & 3) == 1, folded[1:2], folded[2:3]))
    wide = jnp.where(keep_top, wide, 0.0)
    wide_h, wide_l = split(wide)
    rx3[0] = dot(wide_h, slot_z) + dot(wide_l, slot_z)
    copies_t3 = top_copies(2, rx3.at[0], rx3)
    for copy in copies_t3:
        copy.start()

    for copy in copies_t1 + copies_a + copies_far + copies_t2:
        copy.wait_send()

    for group in (0, 1, -1):
        for copy, (dx, dy) in zip(copies_b, NEAR + [(-1, 0), (1, 0)]):
            if dx == group:
                copy.wait_recv()
        first = xd[group].start
        if group != 0:
            for x in range(8):
                rows = edge_rows[0 if group == -1 else 1, 2 * x : 2 * x + 8, :]
                fext[first + x, 16:24, :] = jnp.where(slot_at < 2, rows, 0.0)
        half = xd[group].size // 2

        def level1_y(step, carry, first=first, half=half):
            for u in range(half):
                smooth_y(fext, band_y1, v1, first + step * half + u)
            return carry

        lax.fori_loop(0, 2, level1_y, 0)

    pairs, beyond = [], jnp.zeros((32, 160), F32)
    for first in (0, 2):
        smooth_x(v1, y1, 1, 10, (first, first + 1))
        part = slice(first * 128, first * 128 + 256)
        hi, lo = split(y1[:, part])
        beyond = beyond + dot(edge_h[:, part], hi, nt) + dot(edge_h[:, part], lo, nt) + dot(edge_l[:, part], hi, nt)
        pairs.append((hi, lo))
    zs1[:, 0:160] = beyond
    y1h = jnp.concatenate([hi for hi, _ in pairs], axis=1)
    y1l = jnp.concatenate([lo for _, lo in pairs], axis=1)
    copies_z1 = [
        remote(zs1.at[pl.ds(0, 16)], zr1.at[pl.ds(0, 16)], z_send.at[2], z_recv.at[2], left),
        remote(zs1.at[pl.ds(16, 16)], zr1.at[pl.ds(16, 16)], z_send.at[3], z_recv.at[3], right),
    ]
    for copy in copies_z1:
        copy.start()
    level1 = dot(y1h, main_h) + dot(y1h, main_l) + dot(y1l, main_h)

    lh, ll = split(level1)
    from_cells = table[0:256, 0:160]
    potential = out[...].reshape(256, 128) + dot(from_cells, lh) + dot(from_cells, ll)

    for copy in copies_z0:
        copy.wait_recv()
    tn = ((0,), (0,))
    zh, zl = split(zr0[...])
    out[...] = (potential + dot(zh, c_sel, tn) + dot(zl, c_sel, tn)).reshape(16, 16, 128)

    for copy in copies_b + copies_z0 + copies_t3 + copies_z1:
        copy.wait_send()

    for copy in copies_t3:
        copy.wait_recv()
    total = rx3[0]
    for o in range(1, nz):
        total = total + rx3[o]
    top_h, top_l = split(dot3(total, top_mix, nt))

    for copy in copies_z1:
        copy.wait_recv()
    zh, zl = split(zr1[...])
    side_h, side_l = split((dot(zh, c_edge, tn) + dot(zl, c_edge, tn))[0:160])
    late = dot(table[0:256, 0:208], jnp.concatenate([side_h, top_h, top_h, top_l], axis=0)) + dot(from_cells, side_l)
    out[...] = out[...] + late.reshape(16, 16, 128)


def solution(mesh):
    sizes = tuple(mesh.shape[axis] for axis in AXES)
    packed = tables()

    def local(charges, exponents, amplitudes, top_x, top_y, top_z):
        vmem = pl.BlockSpec(memory_space=pltpu.VMEM)
        hbm = pl.BlockSpec(memory_space=pltpu.HBM)
        return pl.pallas_call(
            functools.partial(kernel, sizes),
            out_shape=jax.ShapeDtypeStruct(charges.shape, F32),
            in_specs=[hbm] * 7,
            out_specs=vmem,
            scratch_shapes=[
                pltpu.SMEM((2, TERMS), F32),
                pltpu.SMEM((2, TERMS), F32),
                pltpu.SMEM(top_x.shape, F32),
                pltpu.SMEM(top_y.shape, F32),
                pltpu.VMEM(top_z.shape, F32),
                pltpu.VMEM(packed.shape, BF16),
                pltpu.SemaphoreType.DMA((7,)),
                pltpu.VMEM((32, 32, 128), F32),
                pltpu.VMEM((32, 64, 128), F32),
                pltpu.VMEM((256, 512), F32),
                pltpu.VMEM((26, 32, 128), F32),
                pltpu.VMEM((10, 8, 128), F32),
                pltpu.VMEM((2, 16, 128), F32),
                pltpu.VMEM((2, 24, 128), F32),
                pltpu.VMEM((26, 64, 128), F32),
                pltpu.VMEM((160, 512), F32),
                pltpu.VMEM((8, 1, 128), F32),
                pltpu.VMEM((8, 1, 128), F32),
                pltpu.VMEM((8, 16, 128), F32),
                pltpu.VMEM((16, 256), F32),
                pltpu.VMEM((32, 256), F32),
                pltpu.VMEM((16, 256), F32),
                pltpu.VMEM((32, 256), F32),
                pltpu.VMEM((72, 8, 128), F32),
                pltpu.VMEM((8, 8, 128), F32),
                pltpu.SemaphoreType.DMA((16,)),
                pltpu.SemaphoreType.DMA((16,)),
                pltpu.SemaphoreType.DMA((10,)),
                pltpu.SemaphoreType.DMA((10,)),
                pltpu.SemaphoreType.DMA((24,)),
                pltpu.SemaphoreType.DMA((24,)),
                pltpu.SemaphoreType.DMA((4,)),
                pltpu.SemaphoreType.DMA((4,)),
            ],
            compiler_params=pltpu.CompilerParams(
                collective_id=0, has_side_effects=True, vmem_limit_bytes=40 * 2**20
            ),
        )(*[
            pltpu.with_memory_space_constraint(v, pltpu.HBM)
            for v in (charges, exponents, amplitudes, top_x, top_y, top_z, jnp.asarray(packed))
        ])

    in_specs = (P("gx", "gy", "gz"), P(), P(), P(), P(), P())
    return jax.shard_map(local, mesh=mesh, in_specs=in_specs, out_specs=P("gx", "gy", "gz"), check_vma=False)
```
